512 devices in a mesh: grp: 8 (over y_lo, x), ep: 64 (over y_hi, z, core).
Axes of the slice: x: 4, y: 8 (y_hi: 4, y_lo: 2; y = y_hi * 2 + y_lo), z: 8, core: 2. Of those that a mesh axis runs over, the one named last changes fastest.
Arguments:
- tokens: bfloat16 [256, 6144], P('grp', 'ep'), may hold values from -6 to 6
- query_weight: bfloat16 [6144, 8192], P('grp', 'ep'), may hold values from -0.078125 to 0.078125
- key_weight: bfloat16 [6144, 8192], P('grp', 'ep'), may hold values from -0.078125 to 0.078125
- value_weight: bfloat16 [6144, 8192], P('grp', 'ep'), may hold values from -0.078125 to 0.078125
- output_weight: bfloat16 [6144, 8192], P('grp', 'ep'), may hold values from -0.0625 to 0.0625
- gate_weight: bfloat16 [6144, 18432], P('grp', 'ep'), may hold values from -0.078125 to 0.078125
- up_weight: bfloat16 [6144, 18432], P('grp', 'ep'), may hold values from -0.078125 to 0.078125
- down_weight: bfloat16 [6144, 18432], P('grp', 'ep'), may hold values from -0.0625 to 0.0625
- router_weight: bfloat16 [6144, 32], replicated, may hold values from -0.078125 to 0.078125
- attn_gain: float32 [6144], replicated, may hold values from 0.1 to 1.9
- expert_gain: float32 [6144], replicated, may hold values from 0.1 to 1.9
- decay_rate: float32 [64], P('ep'), may hold values from 0.02 to 2
- states: float32 [256, 64, 128, 128], P('grp', 'ep'), may hold values from -12 to 12
- expert_ids: int32 [256, 2], P('grp'), may hold values from 0 to 31, all different within a row
- row_slot: int32 [256], P('grp'), may hold values from 0 to 31, as said below
- migration: int32 [16, 3], replicated, may hold values from 0 to 31, as said below
Outputs:
- layer_out: bfloat16 [256, 6144], P('grp', 'ep')
The draws below stay inside these ranges and needn't reach their ends.
Inputs may be any that keep to these rules, and one draw needn't show every extreme that they name: Within each group's 32 rows, row_slot is a permutation of 0 to 31. `migration`: column 0 names a group below the last, column 1 any slot, column 2 distinct slots of the last group.
All inputs are finite; a program needn't handle non-finite values.
Results may differ from the reference program's by a relative error of at most 0.017.
Values may be sent and summed in bfloat16 or wider, within the bound.
No kernel may reach another device: no remote copies, remote signals or barrier semaphores. Data moves between devices by JAX's collectives and lax.ppermute only.
A program may use at most 64 MiB of HBM per device.

```python
import math
import jax
import jax.numpy as jnp
from jax import lax

D = 6144
DH = 128
FF = 9216
EXPERTS = 32
EXP_WIN = 2
SLOTS = 32
MIG = 16
HEADS = 64
ROWS = 256


def draw_row_slot(key, part):
    key = jax.random.fold_in(key, 11)
    group_keys = jax.random.split(key, ROWS // SLOTS)
    orders = jax.vmap(lambda one_key: jax.random.permutation(one_key, SLOTS))(group_keys)
    return orders.reshape(-1).astype(jnp.int32)


def draw_migration(key, part):
    key = jax.random.fold_in(key, 23)
    first_key, second_key, third_key = jax.random.split(key, 3)
    sources = jax.random.randint(first_key, (MIG,), 0, ROWS // SLOTS - 1).astype(jnp.int32).at[0].set(0)
    source_slots = jax.random.randint(second_key, (MIG,), 0, SLOTS).astype(jnp.int32).at[0].set(SLOTS - 1)
    targets = jax.random.permutation(third_key, SLOTS)[:MIG].astype(jnp.int32)
    return jnp.stack([sources, source_slots, targets], axis=1)


def block_levels(stream_key, dims, pieces, low, high):
    loudness, own = 1.0, jax.random.fold_in(stream_key, 6)
    for position, blocks in pieces:
        steps = jnp.exp(jax.random.uniform(jax.random.fold_in(own, position), (blocks,), jnp.float32, low / len(pieces), high / len(pieces)))
        loudness = loudness * jnp.repeat(steps, dims[position] // blocks).reshape([-1 if axis == position else 1 for axis in range(len(dims))])
    return loudness


def distinct(own_key, rows, amount, top, lift):
    sequence = jax.random.permutation(jax.random.fold_in(own_key, 1), amount)
    pull = sequence
    for power in range(3):
        pull = pull * pull // amount
    pull = pull * lift // amount
    chance = jax.random.randint(jax.random.fold_in(own_key, 2), (rows, amount), 0, 4096) + pull
    fixed_rows = jax.random.permutation(jax.random.fold_in(own_key, 3), rows)[jnp.arange(amount) % rows]
    chance = jnp.where(jnp.arange(rows)[:, None] == fixed_rows[None, :], 1 << 14, chance)
    priority = chance * amount + jnp.arange(amount)
    return lax.top_k(priority.astype(jnp.int32), top)[1].astype(jnp.int32)


def centred(rng, extent, spread, bound, cuts=(), held_as=jnp.bfloat16):
    array = spread * jax.random.normal(rng, extent, jnp.float32)
    if cuts:
        array = array * block_levels(rng, extent, cuts, -0.22, 0.18)
    return jnp.clip(array, -bound, bound).astype(held_as)


def setup_inputs(seed: int = 0) -> dict:
    key_of = jax.random.split(jax.random.key(seed), 17)
    return {
        "tokens": centred(key_of[0], (ROWS, D), 1.0, 6.0, ((0, 8), (1, 64))),
        "query_weight": centred(key_of[1], (D, HEADS * DH), D ** -0.5, 0.078125, ((0, 8), (1, 64))),
        "key_weight": centred(key_of[2], (D, HEADS * DH), D ** -0.5, 0.078125, ((0, 8), (1, 64))),
        "value_weight": centred(key_of[3], (D, HEADS * DH), D ** -0.5, 0.078125, ((0, 8), (1, 64))),
        "output_weight": centred(key_of[4], (D, HEADS * DH), (HEADS * DH) ** -0.5, 0.0625, ((0, 8), (1, 64))),
        "gate_weight": centred(key_of[5], (D, EXP_WIN * FF), D ** -0.5, 0.078125, ((0, 8), (1, 64))),
        "up_weight": centred(key_of[6], (D, EXP_WIN * FF), D ** -0.5, 0.078125, ((0, 8), (1, 64))),
        "down_weight": centred(key_of[7], (D, EXP_WIN * FF), FF ** -0.5, 0.0625, ((0, 8), (1, 64))),
        "router_weight": centred(key_of[8], (D, EXPERTS), D ** -0.5, 0.078125),
        "attn_gain": jnp.clip(1.0 + 0.18 * jax.random.normal(key_of[9], (D,), jnp.float32), 0.1, 1.9),
        "expert_gain": jnp.clip(1.0 + 0.18 * jax.random.normal(key_of[10], (D,), jnp.float32), 0.1, 1.9),
        "decay_rate": jnp.clip(jnp.exp(math.log(2.0) - 4.6051702 * jax.random.uniform(key_of[11], (HEADS,), jnp.float32) ** block_levels(key_of[11], (HEADS,), ((0, 64),), -0.2, 0.2)), 0.02, 2.0),
        "states": centred(key_of[12], (ROWS, HEADS, DH, DH), 2.0, 12.0, ((0, 8), (1, 64)), jnp.float32),
        "expert_ids": distinct(key_of[13], ROWS, EXPERTS, 2, 512),
        "row_slot": draw_row_slot(jax.random.fold_in(key_of[16], 71), 0),
        "migration": draw_migration(jax.random.fold_in(key_of[16], 71), 0),
    }


def normed(rows, gain):
    wide = rows.astype(jnp.float32)
    return wide * lax.rsqrt(lax.optimization_barrier(jnp.mean(wide * wide, axis=-1, keepdims=True)) + 1e-06) * gain

def reference(tokens, query_weight, key_weight, value_weight, output_weight, gate_weight, up_weight, down_weight, router_weight, attn_gain, expert_gain, decay_rate, states, expert_ids, row_slot, migration):
    group_count = ROWS // SLOTS
    attn_in = normed(tokens, attn_gain).astype(jnp.bfloat16)
    query_rows = jax.nn.silu(jnp.dot(attn_in, query_weight, preferred_element_type=jnp.float32)).reshape(group_count, SLOTS, HEADS, DH)
    key_rows = jax.nn.silu(jnp.dot(attn_in, key_weight, preferred_element_type=jnp.float32)).reshape(group_count, SLOTS, HEADS, DH)
    value_rows = jax.nn.silu(jnp.dot(attn_in, value_weight, preferred_element_type=jnp.float32)).reshape(group_count, SLOTS, HEADS, DH)
    source_index = (migration[:, 0] * SLOTS + migration[:, 1]).astype(jnp.int32)
    moved = states[source_index]
    retain = jnp.exp(-decay_rate)
    grouped_states = states.reshape(group_count, SLOTS, HEADS, DH, DH)
    grouped_slots = row_slot.reshape(group_count, SLOTS)
    group_ids = jnp.arange(group_count, dtype=jnp.int32)

    def one_group(items):
        query_g, key_g, value_g, slots_g, stored, gid = items
        updated = stored.at[migration[:, 2]].set(moved)
        stored = jnp.where(gid == group_count - 1, updated, stored)
        current = stored[slots_g]
        fresh = retain[None, :, None, None] * current + key_g[:, :, :, None] * value_g[:, :, None, :]
        return jnp.einsum('shi,shij->shj', query_g, fresh, precision=lax.Precision.HIGHEST)
    mixed = lax.map(one_group, (query_rows, key_rows, value_rows, grouped_slots, grouped_states, group_ids))
    mixed = mixed.reshape(ROWS, HEADS, DH)
    heads_out = (mixed * lax.rsqrt(lax.optimization_barrier(jnp.mean(mixed * mixed, axis=-1, keepdims=True)) + 1e-06)).astype(jnp.bfloat16).reshape(ROWS, HEADS * DH)
    attn_sum = jnp.dot(heads_out, output_weight.T, preferred_element_type=jnp.float32)
    resid = (tokens.astype(jnp.float32) + attn_sum).astype(jnp.bfloat16)
    expert_in = normed(resid, expert_gain).astype(jnp.bfloat16)
    logits = jnp.dot(expert_in, router_weight, preferred_element_type=jnp.float32)
    chosen = jnp.take_along_axis(logits, expert_ids, axis=1)
    lifted = jax.nn.sigmoid(chosen)
    shares = lifted / lax.optimization_barrier(jnp.sum(lifted, axis=1, keepdims=True))
    expert_range = jnp.arange(EXP_WIN, dtype=jnp.int32)
    weight_table = lax.optimization_barrier(jnp.sum(jnp.where(expert_ids[:, :, None] == expert_range[None, None, :], shares[:, :, None], 0.0), axis=1))
    gate = jnp.dot(expert_in, gate_weight, preferred_element_type=jnp.float32)
    upper = jnp.dot(expert_in, up_weight, preferred_element_type=jnp.float32)
    hidden = (jax.nn.silu(gate) * upper).astype(jnp.bfloat16)
    hidden_blocks = jnp.transpose(hidden.reshape(ROWS, EXP_WIN, FF), (1, 0, 2))
    down_blocks = jnp.transpose(down_weight.reshape(D, EXP_WIN, FF), (1, 0, 2))

    def add_expert(total, items):
        hidden_e, down_e, weight_e = items
        product = lax.dot_general(hidden_e, down_e, (((1,), (1,)), ((), ())), preferred_element_type=jnp.float32)
        return (total + weight_e[:, None] * product, None)
    expert_out, _ = lax.scan(add_expert, jnp.zeros((ROWS, D), jnp.float32), (hidden_blocks, down_blocks, weight_table.T))
    return (resid.astype(jnp.float32) + expert_out).astype(jnp.bfloat16)
```

```python
import jax
import jax.numpy as jnp
from jax import lax
from jax.experimental import pallas as pl
from jax.experimental.pallas import tpu as pltpu
from jax.sharding import PartitionSpec as P

BF16, F32 = jnp.bfloat16, jnp.float32
GRP = ("yl", "x")
EPA = ("yh", "zh", "zl", "c")
CHIPS = ("yh", "zh", "zl")
PLANE = ("yl", "x", "yh", "zh")
SWAP = [(g * 8 + h, h * 8 + g) for g in range(8) for h in range(8)]
CORES = [(0, 1), (1, 0)]
D, FF, DH = 6144, 9216, 128
EPS = 1e-6
CHUNK, SLICE, SLOTS, MIG, UNITS = 96, 768, 32, 16, 288
VMEM = pl.BlockSpec(memory_space=pltpu.VMEM)
SMEM = pl.BlockSpec(memory_space=pltpu.SMEM)


def call(kernel, outs, ins, name, smem=(), limit=48 << 20):
    specs = [SMEM if i in smem else VMEM for i in range(len(ins))]
    return pl.pallas_call(
        kernel,
        out_shape=outs,
        in_specs=specs,
        out_specs=jax.tree.map(lambda _: VMEM, outs),
        compiler_params=pltpu.CompilerParams(vmem_limit_bytes=limit),
        name=name,
    )(*ins)


def shape(dims, dtype):
    return jax.ShapeDtypeStruct(dims, dtype)


def dot_nt(left, right):
    return lax.dot_general(left, right, (((1,), (1,)), ((), ())), preferred_element_type=F32)


def silu(x):
    return x * (1.0 / (1.0 + jnp.exp(-x)))


def sort_kernel(tokens_ref, slot_row_ref, out_ref):
    place = lax.broadcasted_iota(jnp.int32, (SLOTS, SLOTS), 0) == slot_row_ref[...]
    out_ref[...] = jnp.dot(
        place.astype(F32).astype(BF16), tokens_ref[...], preferred_element_type=F32
    ).astype(BF16)


def features(own_ref, other_ref, gain_ref, where_ref):
    group, core = where_ref[0], where_ref[1]
    for pair in range(4):
        for ref, side in ((own_ref, core), (other_ref, 1 - core)):
            chunk = 2 * pair + side
            x = ref[:, pair].reshape(8 * SLOTS, CHUNK).astype(F32)
            scaled = (x * gain_ref[pl.ds(group * 8 + chunk, 1), :]).astype(BF16)
            yield pl.multiple_of(chunk * CHUNK, 32), scaled, jnp.sum(x * x, axis=1, keepdims=True)


def stats_lanes(total, lane):
    high = total.astype(BF16).astype(F32)
    at = lax.broadcasted_iota(jnp.int32, (total.shape[0], 128), 1)
    return jnp.where(at == lane, high, jnp.where(at == lane + 1, total - high, 0.0))


def qkv_kernel(own_ref, other_ref, q_ref, k_ref, v_ref, gain_ref, target_ref, where_ref, out_ref):
    q = k = v = total = 0.0
    for at, scaled, squares in features(own_ref, other_ref, gain_ref, where_ref):
        rows = pl.ds(at, CHUNK)
        q += jnp.dot(scaled, q_ref[rows, :], preferred_element_type=F32)
        k += jnp.dot(scaled, k_ref[rows, :], preferred_element_type=F32)
        v += jnp.dot(scaled, v_ref[rows, :], preferred_element_type=F32)
        total += squares
    pick = lax.broadcasted_iota(jnp.int32, (MIG, SLOTS), 1) == target_ref[...]
    pick = pick.astype(F32).astype(BF16)
    for i, part in enumerate((q, k, v, stats_lanes(total, 0))):
        part = part.astype(BF16)
        lanes = slice(128 * i, 128 * i + 128)
        out_ref[:, :SLOTS, lanes] = part.reshape(8, SLOTS, 128)
        moved = jnp.dot(pick, part[7 * SLOTS :], preferred_element_type=F32).astype(BF16)
        for d in range(8):
            out_ref[d, SLOTS:, lanes] = moved


def attention_kernel(got_ref, states_ref, source_ref, decay_ref, migration_ref, where_ref, out_ref, o_ref):
    total = got_ref[0].astype(F32)
    for i in range(1, 8):
        total += got_ref[i].astype(F32)
    squares = total[:, 384:385] + total[:, 385:386]
    scale = lax.rsqrt(squares * (1.0 / D) + EPS)
    q, k, v = (silu(scale * total[:, 128 * i : 128 * i + 128]) for i in range(3))
    rows = SLOTS + MIG
    turned = jnp.concatenate([q, jnp.zeros((128 - rows, 128), F32)], axis=0).T
    for s in range(SLOTS):
        o_ref[s : s + 1, :] = jnp.sum(turned[:, s : s + 1] * states_ref[s], axis=0, keepdims=True)
    for m in range(MIG):
        s = SLOTS + m
        o_ref[s : s + 1, :] = jnp.sum(
            turned[:, s : s + 1] * states_ref[migration_ref[m, 1]], axis=0, keepdims=True
        )
    retain = jnp.exp(-decay_ref[...])
    mixed = retain * o_ref[...] + jnp.sum(q * k, axis=1, keepdims=True) * v
    heads = mixed * lax.rsqrt(jnp.mean(mixed * mixed, axis=1, keepdims=True) + EPS)
    here = source_ref[...] == where_ref[0]
    own = heads[:SLOTS].astype(BF16)
    moved = jnp.where(here, heads[SLOTS:], 0.0).astype(BF16)
    for d in range(8):
        out_ref[d, :SLOTS] = own
        out_ref[d, SLOTS:] = moved


def output_kernel(got_ref, weight_ref, target_ref, where_ref, keep_ref, send_ref):
    core = where_ref[1]
    moved = got_ref[0, SLOTS:].astype(F32)
    for i in range(1, 8):
        moved += got_ref[i, SLOTS:].astype(F32)
    place = lax.broadcasted_iota(jnp.int32, (SLOTS, MIG), 0) == target_ref[...]
    place = place.astype(F32)
    landed = jnp.dot(place.astype(BF16), moved.astype(BF16), preferred_element_type=F32)
    taken = jnp.sum(place, axis=1, keepdims=True) > 0.0
    last = jnp.where(taken, landed, got_ref[7, :SLOTS].astype(F32)).astype(BF16)
    rows = jnp.concatenate([got_ref[:7, :SLOTS].reshape(7 * SLOTS, DH), last], axis=0)
    for pair in range(4):
        for ref, side in ((keep_ref, core), (send_ref, 1 - core)):
            at = pl.multiple_of((2 * pair + side) * CHUNK, 32)
            part = dot_nt(rows, weight_ref[pl.ds(at, CHUNK), :])
            ref[:, pair] = part.reshape(8, SLOTS, CHUNK).astype(ref.dtype)


def resid_kernel(got_ref, tokens_ref, resid_ref, spread_ref):
    total = got_ref[0].astype(F32)
    for i in range(1, 32):
        total += got_ref[i].astype(F32)
    resid = (tokens_ref[...].astype(F32) + total).astype(BF16)
    resid_ref[...] = resid
    for i in range(32):
        spread_ref[i] = resid


def gate_kernel(own_ref, other_ref, gate_ref, up_ref, tail_ref, gain_ref, where_ref, out_ref):
    gate = up = tail = total = 0.0
    for at, scaled, squares in features(own_ref, other_ref, gain_ref, where_ref):
        rows = pl.ds(at, CHUNK)
        gate += jnp.dot(scaled, gate_ref[rows, :256], preferred_element_type=F32)
        up += jnp.dot(scaled, up_ref[rows, :256], preferred_element_type=F32)
        tail += jnp.dot(scaled, tail_ref[rows, :], preferred_element_type=F32)
        total += squares
    tail += stats_lanes(total, 96)
    out_ref[:, :, :256] = gate.astype(BF16).reshape(8, SLOTS, 256)
    out_ref[:, :, 256:512] = up.astype(BF16).reshape(8, SLOTS, 256)
    out_ref[:, :, 512:] = tail.astype(BF16).reshape(8, SLOTS, 128)


def expert_kernel(got_ref, down_ref, ids_ref, slot_row_ref, where_ref, keep_ref, send_ref):
    core, expert = where_ref[1], where_ref[2]
    total = got_ref[0].astype(F32)
    for i in range(1, 8):
        total += got_ref[i].astype(F32)
    tail = total[:, 512:]
    scale = lax.rsqrt((tail[:, 96:97] + tail[:, 97:98]) * (1.0 / D) + EPS)
    main = (silu(scale * total[:, :256]) * (scale * total[:, 256:512])).astype(BF16)
    rest = (silu(scale * tail[:, :32]) * (scale * tail[:, 32:64])).astype(BF16)
    logits = scale * tail[:, 64:96]
    place = lax.broadcasted_iota(jnp.int32, (SLOTS, SLOTS), 0) == slot_row_ref[...]
    ids = jnp.dot(
        place.astype(F32).astype(BF16), ids_ref[...].astype(F32).astype(BF16), preferred_element_type=F32
    )
    ids = (ids + 0.5).astype(jnp.int32)
    at = lax.broadcasted_iota(jnp.int32, (SLOTS, 32), 1)
    lifted = []
    for i in range(2):
        chosen = jnp.sum(jnp.where(at == ids[:, i : i + 1], logits, 0.0), axis=1, keepdims=True)
        lifted.append(1.0 / (1.0 + jnp.exp(-chosen)))
    mine = jnp.where(ids[:, 0:1] == expert, lifted[0], 0.0)
    mine += jnp.where(ids[:, 1:2] == expert, lifted[1], 0.0)
    share = mine / (lifted[0] + lifted[1])
    hidden = jnp.concatenate([main, rest], axis=1)
    for chip in range(32):
        for ref, side in ((keep_ref, core), (send_ref, 1 - core)):
            row = pl.multiple_of((2 * chip + side) * CHUNK, 32)
            part = dot_nt(hidden, down_ref[pl.ds(row, CHUNK), :])
            ref[chip] = (part * share).astype(ref.dtype)


def final_kernel(got_ref, resid_ref, slot_ref, out_ref):
    total = got_ref[0].astype(F32)
    for i in range(1, 32):
        total += got_ref[i].astype(F32)
    out = (resid_ref[...].astype(F32) + total).astype(BF16)
    place = lax.broadcasted_iota(jnp.int32, (SLOTS, SLOTS), 1) == slot_ref[...]
    out_ref[...] = jnp.dot(
        place.astype(F32).astype(BF16), out, preferred_element_type=F32
    ).astype(BF16)


def exchange(x, axes):
    return lax.all_to_all(x, axes, 0, 0)


def shards(
    tokens,
    query_weight,
    key_weight,
    value_weight,
    output_weight,
    gate_weight,
    up_weight,
    down_weight,
    router_weight,
    attn_gain,
    expert_gain,
    decay_rate,
    states,
    expert_ids,
    row_slot,
    migration,
):
    group = lax.axis_index(GRP).astype(jnp.int32)
    core = lax.axis_index("c").astype(jnp.int32)
    device = lax.axis_index(EPA).astype(jnp.int32)
    where = jnp.stack([group, core, device * UNITS // FF])
    slot_row, slot_column = row_slot[None, :], row_slot[:, None]

    down_full = lax.all_gather(down_weight, GRP, axis=0, tiled=True)

    ordered = call(sort_kernel, shape((SLOTS, CHUNK), BF16), (tokens, slot_row), "sort_rows")
    block = lax.ppermute(ordered, PLANE, SWAP)

    router = lax.dynamic_slice_in_dim(router_weight, group * SLICE, SLICE, 0)
    tail = jnp.concatenate(
        [gate_weight[:, 256:], up_weight[:, 256:], router, jnp.zeros((SLICE, 32), BF16)], axis=1
    )
    attn_gain, expert_gain = attn_gain.reshape(64, CHUNK), expert_gain.reshape(64, CHUNK)

    def gather(spread):
        own = exchange(spread, CHIPS)
        other = lax.ppermute(own, "c", CORES)
        return own.reshape(8, 4, SLOTS, CHUNK), other.reshape(8, 4, SLOTS, CHUNK)

    def scatter(keep, send):
        got = lax.ppermute(send, "c", CORES)
        both = (keep + got.astype(F32)).astype(BF16)
        return exchange(both.reshape(32, SLOTS, CHUNK), CHIPS)

    own, other = gather(jnp.broadcast_to(block[None], (32, SLOTS, CHUNK)))
    parts = call(
        qkv_kernel,
        shape((8, SLOTS + MIG, 512), BF16),
        (own, other, query_weight, key_weight, value_weight, attn_gain, migration[:, 2:3], where),
        "qkv_parts",
        smem=(7,),
    )
    parts = exchange(parts, GRP)
    heads = pl.pallas_call(
        attention_kernel,
        out_shape=shape((8, SLOTS + MIG, DH), BF16),
        in_specs=[VMEM, VMEM, VMEM, VMEM, SMEM, SMEM],
        out_specs=VMEM,
        scratch_shapes=[pltpu.VMEM((SLOTS + MIG, DH), F32)],
        compiler_params=pltpu.CompilerParams(vmem_limit_bytes=48 << 20),
        name="attention",
    )(parts, states[:, 0], migration[:, 0:1], decay_rate[None], migration, where)
    heads = exchange(heads, GRP)
    keep, send = call(
        output_kernel,
        (shape((8, 4, SLOTS, CHUNK), F32), shape((8, 4, SLOTS, CHUNK), BF16)),
        (heads, output_weight, migration[:, 2][None, :], where),
        "output_parts",
        smem=(3,),
    )
    resid, spread = call(
        resid_kernel,
        (shape((SLOTS, CHUNK), BF16), shape((32, SLOTS, CHUNK), BF16)),
        (scatter(keep, send), block),
        "resid",
    )
    own, other = gather(spread)
    resid = lax.ppermute(resid, PLANE, SWAP)
    parts = call(
        gate_kernel,
        shape((8, SLOTS, 640), BF16),
        (own, other, gate_weight, up_weight, tail, expert_gain, where),
        "gate_parts",
        smem=(6,),
    )
    parts = exchange(parts, GRP)
    keep, send = call(
        expert_kernel,
        (shape((32, SLOTS, CHUNK), F32), shape((32, SLOTS, CHUNK), BF16)),
        (parts, down_full, expert_ids, slot_row, where),
        "expert_parts",
        smem=(4,),
    )
    return call(
        final_kernel,
        shape((SLOTS, CHUNK), BF16),
        (scatter(keep, send), resid, slot_column),
        "layer_out",
    )


def solution(mesh):
    fine = jax.sharding.Mesh(
        mesh.devices.reshape(2, 4, 4, 2, 4, 2), ("yl", "x", "yh", "zh", "zl", "c")
    )
    both = P(GRP, EPA)
    placed = (both,) * 8 + (
        P(),
        P(),
        P(),
        P(EPA),
        P(GRP, EPA, None, None),
        P(GRP, None),
        P(GRP),
        P(),
    )
    return jax.shard_map(shards, mesh=fine, in_specs=placed, out_specs=both, check_vma=False)
```

```python
import jax
import jax.numpy as jnp
from jax import lax
from jax.experimental import pallas as pl
from jax.experimental.pallas import tpu as pltpu
from jax.sharding import PartitionSpec as P

BF16, F32 = jnp.bfloat16, jnp.float32
GRP = ("yl", "x")
EPA = ("yh", "zh", "zl", "c")
CHIPS = ("yh", "zh", "zl")
CORES = [(0, 1), (1, 0)]
D, FF, DH = 6144, 9216, 128
EPS = 1e-6
CHUNK, SLICE, SLOTS, MIG, UNITS = 96, 768, 32, 16, 288
VMEM = pl.BlockSpec(memory_space=pltpu.VMEM)
HBM = pl.BlockSpec(memory_space=pltpu.HBM)
SMEM = pl.BlockSpec(memory_space=pltpu.SMEM)


def call(kernel, outs, ins, name, smem=(), limit=16 << 20):
    specs = [SMEM if i in smem else VMEM for i in range(len(ins))]
    return pl.pallas_call(
        kernel,
        out_shape=outs,
        in_specs=specs,
        out_specs=jax.tree.map(lambda _: VMEM, outs),
        compiler_params=pltpu.CompilerParams(vmem_limit_bytes=limit),
        name=name,
    )(*ins)


def shape(dims, dtype):
    return jax.ShapeDtypeStruct(dims, dtype)


def dot_nt(left, right):
    return lax.dot_general(left, right, (((1,), (1,)), ((), ())), preferred_element_type=F32)


def silu(x):
    return x * (1.0 / (1.0 + jnp.exp(-x)))


def fetch(pairs, sems):
    copies = [pltpu.make_async_copy(a, b, sems.at[i]) for i, (a, b) in enumerate(pairs)]
    for copy in copies:
        copy.start()
    return copies


def sort_kernel(tokens_ref, slot_ref, out_ref, held_ref, row_ref, sems):
    for copy in fetch(((tokens_ref, held_ref), (slot_ref, row_ref)), sems):
        copy.wait()
    place = lax.broadcasted_iota(jnp.int32, (SLOTS, SLOTS), 0) == row_ref[...]
    rows = jnp.dot(
        place.astype(F32).astype(BF16), held_ref[...], preferred_element_type=F32
    ).astype(BF16)
    for i in range(32):
        out_ref[i] = rows


def slice_rows(own_ref, other_ref, gain_ref, where_ref):
    group, first = where_ref[0], where_ref[1] == 0
    pieces = []
    for pair in range(4):
        own = own_ref[:, pair].reshape(8 * SLOTS, CHUNK).astype(F32)
        other = other_ref[:, pair].reshape(8 * SLOTS, CHUNK).astype(F32)
        pieces += [jnp.where(first, own, other), jnp.where(first, other, own)]
    rows = jnp.concatenate(pieces, axis=1)
    scaled = [
        (rows[:, 128 * j : 128 * j + 128] * gain_ref[pl.ds(6 * group + j, 1), :]).astype(BF16)
        for j in range(6)
    ]
    return jnp.concatenate(scaled, axis=1), jnp.sum(rows * rows, axis=1, keepdims=True)


def stats_lanes(total, lane):
    high = total.astype(BF16).astype(F32)
    at = lax.broadcasted_iota(jnp.int32, (total.shape[0], 128), 1)
    return jnp.where(at == lane, high, jnp.where(at == lane + 1, total - high, 0.0))


def qkv_kernel(
    own_ref, other_ref, q_ref, k_ref, v_ref, gain_ref, target_ref, where_ref, out_ref, scale_ref, held_ref, sems
):
    pairs = [(ref, held_ref.at[i]) for i, ref in enumerate((q_ref, k_ref, v_ref))]
    gain, *copies = fetch([(gain_ref, scale_ref), *pairs], sems)
    gain.wait()
    rows, total = slice_rows(own_ref, other_ref, scale_ref, where_ref)
    parts = []
    for i, copy in enumerate(copies):
        copy.wait()
        parts.append(jnp.dot(rows, held_ref[i], preferred_element_type=F32))
    pick = lax.broadcasted_iota(jnp.int32, (MIG, SLOTS), 1) == target_ref[...]
    pick = pick.astype(F32).astype(BF16)
    for i, part in enumerate((*parts, stats_lanes(total, 0))):
        part = part.astype(BF16)
        lanes = slice(128 * i, 128 * i + 128)
        out_ref[:, :SLOTS, lanes] = part.reshape(8, SLOTS, 128)
        moved = jnp.dot(pick, part[7 * SLOTS :], preferred_element_type=F32).astype(BF16)
        for d in range(8):
            out_ref[d, SLOTS:, lanes] = moved


def attention_kernel(got_ref, states_ref, source_ref, decay_ref, migration_ref, where_ref, out_ref, o_ref):
    total = got_ref[0].astype(F32)
    for i in range(1, 8):
        total += got_ref[i].astype(F32)
    squares = total[:, 384:385] + total[:, 385:386]
    scale = lax.rsqrt(squares * (1.0 / D) + EPS)
    q, k, v = (silu(scale * total[:, 128 * i : 128 * i + 128]) for i in range(3))
    rows = SLOTS + MIG
    turned = jnp.concatenate([q, jnp.zeros((128 - rows, 128), F32)], axis=0).T
    for s in range(SLOTS):
        o_ref[s : s + 1, :] = jnp.sum(turned[:, s : s + 1] * states_ref[s], axis=0, keepdims=True)
    for m in range(MIG):
        s = SLOTS + m
        o_ref[s : s + 1, :] = jnp.sum(
            turned[:, s : s + 1] * states_ref[migration_ref[m, 1]], axis=0, keepdims=True
        )
    retain = jnp.exp(-decay_ref[...])
    mixed = retain * o_ref[...] + jnp.sum(q * k, axis=1, keepdims=True) * v
    heads = mixed * lax.rsqrt(jnp.mean(mixed * mixed, axis=1, keepdims=True) + EPS)
    here = source_ref[...] == where_ref[0]
    own = heads[:SLOTS].astype(BF16)
    moved = jnp.where(here, heads[SLOTS:], 0.0).astype(BF16)
    for d in range(8):
        out_ref[d, :SLOTS] = own
        out_ref[d, SLOTS:] = moved


def output_kernel(got_ref, weight_ref, target_ref, where_ref, keep_ref, send_ref):
    core = where_ref[1]
    moved = got_ref[0, SLOTS:].astype(F32)
    for i in range(1, 8):
        moved += got_ref[i, SLOTS:].astype(F32)
    place = lax.broadcasted_iota(jnp.int32, (SLOTS, MIG), 0) == target_ref[...]
    place = place.astype(F32)
    landed = jnp.dot(place.astype(BF16), moved.astype(BF16), preferred_element_type=F32)
    taken = jnp.sum(place, axis=1, keepdims=True) > 0.0
    last = jnp.where(taken, landed, got_ref[7, :SLOTS].astype(F32)).astype(BF16)
    rows = jnp.concatenate([got_ref[:7, :SLOTS].reshape(7 * SLOTS, DH), last], axis=0)
    for pair in range(4):
        for ref, side in ((keep_ref, core), (send_ref, 1 - core)):
            at = pl.multiple_of((2 * pair + side) * CHUNK, 32)
            part = dot_nt(rows, weight_ref[pl.ds(at, CHUNK), :])
            ref[:, pair] = part.reshape(8, SLOTS, CHUNK).astype(ref.dtype)


def resid_kernel(got_ref, tokens_ref, where_ref, spread_ref):
    total = got_ref[0].astype(F32)
    for i in range(1, 32):
        total += got_ref[i].astype(F32)
    tokens = tokens_ref[where_ref[3], where_ref[4]]
    resid = (tokens.astype(F32) + total).astype(BF16)
    for i in range(32):
        spread_ref[i] = resid


def gate_kernel(own_ref, other_ref, gate_ref, up_ref, router_ref, gain_ref, where_ref, out_ref):
    rows, total = slice_rows(own_ref, other_ref, gain_ref, where_ref)
    gate = dot_nt(rows, gate_ref[:256])
    up = dot_nt(rows, up_ref[:256])
    at = pl.multiple_of(where_ref[0] * SLICE, SLICE)
    router = router_ref[:, pl.ds(at, SLICE)]
    rest = jnp.concatenate([gate_ref[256:], up_ref[256:], router, jnp.zeros_like(router)], axis=0)
    tail = dot_nt(rows, rest) + stats_lanes(total, 96)
    out_ref[:, :, :256] = gate.astype(BF16).reshape(8, SLOTS, 256)
    out_ref[:, :, 256:512] = up.astype(BF16).reshape(8, SLOTS, 256)
    out_ref[:, :, 512:640] = tail.astype(BF16).reshape(8, SLOTS, 128)
    for d in range(8):
        out_ref[d, :, 640:736] = own_ref[d, where_ref[4]]
        out_ref[d, :, 736:] = jnp.zeros((SLOTS, 32), BF16)


def expert_kernel(
    got_ref, down_ref, ids_ref, slot_row_ref, where_ref, keep_ref, send_ref, resid_ref, held_ref, sems
):
    core, expert = where_ref[1], where_ref[2]
    copies = fetch([(down_ref.at[i], held_ref.at[i]) for i in range(8)], sems)
    resid_ref[...] = got_ref[where_ref[3], :, 640:736]
    total = got_ref[0].astype(F32)
    for i in range(1, 8):
        total += got_ref[i].astype(F32)
    tail = total[:, 512:640]
    scale = lax.rsqrt((tail[:, 96:97] + tail[:, 97:98]) * (1.0 / D) + EPS)
    main = (silu(scale * total[:, :256]) * (scale * total[:, 256:512])).astype(BF16)
    rest = (silu(scale * tail[:, :32]) * (scale * tail[:, 32:64])).astype(BF16)
    logits = scale * tail[:, 64:96]
    place = lax.broadcasted_iota(jnp.int32, (SLOTS, SLOTS), 0) == slot_row_ref[...]
    ids = jnp.dot(
        place.astype(F32).astype(BF16), ids_ref[...].astype(F32).astype(BF16), preferred_element_type=F32
    )
    ids = (ids + 0.5).astype(jnp.int32)
    at = lax.broadcasted_iota(jnp.int32, (SLOTS, 32), 1)
    lifted = []
    for i in range(2):
        chosen = jnp.sum(jnp.where(at == ids[:, i : i + 1], logits, 0.0), axis=1, keepdims=True)
        lifted.append(1.0 / (1.0 + jnp.exp(-chosen)))
    mine = jnp.where(ids[:, 0:1] == expert, lifted[0], 0.0)
    mine += jnp.where(ids[:, 1:2] == expert, lifted[1], 0.0)
    share = mine / (lifted[0] + lifted[1])
    hidden = jnp.concatenate([main, rest], axis=1)
    first = core == 0
    for i, copy in enumerate(copies):
        copy.wait()
        part = jnp.dot(hidden, held_ref[i], preferred_element_type=F32) * share
        for j in range(4):
            even = part[:, 192 * j : 192 * j + 96]
            odd = part[:, 192 * j + 96 : 192 * j + 192]
            keep_ref[4 * i + j] = jnp.where(first, even, odd)
            send_ref[4 * i + j] = jnp.where(first, odd, even).astype(BF16)


def final_kernel(got_ref, resid_ref, slot_ref, out_ref):
    total = got_ref[0].astype(F32)
    for i in range(1, 32):
        total += got_ref[i].astype(F32)
    out = (resid_ref[...].astype(F32) + total).astype(BF16)
    place = lax.broadcasted_iota(jnp.int32, (SLOTS, SLOTS), 1) == slot_ref[...]
    out_ref[...] = jnp.dot(
        place.astype(F32).astype(BF16), out, preferred_element_type=F32
    ).astype(BF16)


def in_hbm(x):
    return pltpu.with_memory_space_constraint(x, pltpu.HBM)


def exchange(x, axes):
    return lax.all_to_all(x, axes, 0, 0)


def shards(
    tokens,
    query_weight,
    key_weight,
    value_weight,
    output_weight,
    gate_weight,
    up_weight,
    down_weight,
    router_weight,
    attn_gain,
    expert_gain,
    decay_rate,
    states,
    expert_ids,
    row_slot,
    migration,
):
    group = lax.axis_index(GRP).astype(jnp.int32)
    core = lax.axis_index("c").astype(jnp.int32)
    device = lax.axis_index(EPA).astype(jnp.int32)
    expert = device * UNITS // FF
    where = jnp.stack([group, core, expert, device // 8, device % 8 // 2])
    slot_row, slot_column = row_slot[None, :], row_slot[:, None]

    attn_gain, expert_gain = attn_gain.reshape(48, 128), expert_gain.reshape(48, 128)

    def scatter(keep, send):
        got = lax.ppermute(send, "c", CORES)
        both = (keep + got.astype(F32)).astype(BF16)
        return exchange(both.reshape(32, SLOTS, CHUNK), CHIPS)

    spread = pl.pallas_call(
        sort_kernel,
        out_shape=shape((32, SLOTS, CHUNK), BF16),
        in_specs=[HBM, HBM],
        out_specs=VMEM,
        scratch_shapes=[
            pltpu.VMEM((SLOTS, CHUNK), BF16),
            pltpu.VMEM((1, SLOTS), jnp.int32),
            pltpu.SemaphoreType.DMA((2,)),
        ],
        name="sorted_rows",
    )(in_hbm(tokens), in_hbm(slot_row))
    own = exchange(exchange(spread, CHIPS).reshape(8, 4, SLOTS, CHUNK), GRP)
    rows_own, other = own, lax.ppermute(own, "c", CORES)
    parts = pl.pallas_call(
        qkv_kernel,
        out_shape=shape((8, SLOTS + MIG, 512), BF16),
        in_specs=[VMEM, VMEM, HBM, HBM, HBM, HBM, VMEM, SMEM],
        out_specs=VMEM,
        scratch_shapes=[
            pltpu.VMEM((48, 128), F32),
            pltpu.VMEM((3, SLICE, DH), BF16),
            pltpu.SemaphoreType.DMA((4,)),
        ],
        compiler_params=pltpu.CompilerParams(vmem_limit_bytes=16 << 20),
        name="qkv_parts",
    )(
        own,
        other,
        in_hbm(query_weight),
        in_hbm(key_weight),
        in_hbm(value_weight),
        in_hbm(attn_gain),
        migration[:, 2:3],
        where,
    )
    parts = exchange(parts, GRP)
    parts, down = lax.optimization_barrier((parts, down_weight.T))
    down_full = lax.all_gather(down, GRP)
    heads = pl.pallas_call(
        attention_kernel,
        out_shape=shape((8, SLOTS + MIG, DH), BF16),
        in_specs=[VMEM, VMEM, VMEM, VMEM, SMEM, SMEM],
        out_specs=VMEM,
        scratch_shapes=[pltpu.VMEM((SLOTS + MIG, DH), F32)],
        compiler_params=pltpu.CompilerParams(vmem_limit_bytes=16 << 20),
        name="attention",
    )(parts, states[:, 0], migration[:, 0:1], decay_rate[None], migration, where)
    heads = exchange(heads, GRP)
    keep, send = call(
        output_kernel,
        (shape((8, 4, SLOTS, CHUNK), F32), shape((8, 4, SLOTS, CHUNK), BF16)),
        (heads, output_weight, migration[:, 2][None, :], where),
        "output_parts",
        smem=(3,),
    )
    spread = call(
        resid_kernel,
        shape((32, SLOTS, CHUNK), BF16),
        (scatter(keep, send), rows_own, where),
        "resid",
        smem=(2,),
    )
    own = exchange(spread, CHIPS).reshape(8, 4, SLOTS, CHUNK)
    other = lax.ppermute(own, "c", CORES)
    parts = call(
        gate_kernel,
        shape((8, SLOTS, 768), BF16),
        (own, other, gate_weight.T, up_weight.T, router_weight.T, expert_gain, where),
        "gate_parts",
        smem=(6,),
    )
    parts = exchange(parts, GRP)
    keep, send, resid = pl.pallas_call(
        expert_kernel,
        out_shape=(
            shape((32, SLOTS, CHUNK), F32),
            shape((32, SLOTS, CHUNK), BF16),
            shape((SLOTS, CHUNK), BF16),
        ),
        in_specs=[VMEM, HBM, VMEM, VMEM, SMEM],
        out_specs=(VMEM, VMEM, VMEM),
        scratch_shapes=[pltpu.VMEM((8, UNITS, SLICE), BF16), pltpu.SemaphoreType.DMA((8,))],
        compiler_params=pltpu.CompilerParams(vmem_limit_bytes=24 << 20),
        name="expert_parts",
    )(parts, in_hbm(down_full), expert_ids, slot_row, where)
    return call(
        final_kernel,
        shape((SLOTS, CHUNK), BF16),
        (scatter(keep, send), resid, slot_column),
        "layer_out",
    )


def solution(mesh):
    fine = jax.sharding.Mesh(
        mesh.devices.reshape(2, 4, 4, 2, 4, 2), ("yl", "x", "yh", "zh", "zl", "c")
    )
    both = P(GRP, EPA)
    placed = (both,) * 8 + (
        P(),
        P(),
        P(),
        P(EPA),
        P(GRP, EPA, None, None),
        P(GRP, None),
        P(GRP),
        P(),
    )
    return jax.shard_map(shards, mesh=fine, in_specs=placed, out_specs=both, check_vma=False)
```

```python
import jax
import jax.numpy as jnp
from jax import lax
from jax.experimental import pallas as pl
from jax.experimental.pallas import tpu as pltpu
from jax.sharding import PartitionSpec as P

BF16, F32 = jnp.bfloat16, jnp.float32
GRP = ("yl", "x")
EPA = ("yh", "zh", "zl", "c")
CHIPS = ("yh", "zh", "zl")
CORES = [(0, 1), (1, 0)]
D, FF, DH = 6144, 9216, 128
EPS = 1e-6
CHUNK, SLICE, SLOTS, MIG, UNITS = 96, 768, 32, 16, 288
VMEM = pl.BlockSpec(memory_space=pltpu.VMEM)
HBM = pl.BlockSpec(memory_space=pltpu.HBM)
SMEM = pl.BlockSpec(memory_space=pltpu.SMEM)


def call(kernel, outs, ins, name, smem=(), limit=16 << 20):
    specs = [SMEM if i in smem else VMEM for i in range(len(ins))]
    return pl.pallas_call(
        kernel,
        out_shape=outs,
        in_specs=specs,
        out_specs=jax.tree.map(lambda _: VMEM, outs),
        compiler_params=pltpu.CompilerParams(vmem_limit_bytes=limit),
        name=name,
    )(*ins)


def shape(dims, dtype):
    return jax.ShapeDtypeStruct(dims, dtype)


def dot_nt(left, right):
    return lax.dot_general(left, right, (((1,), (1,)), ((), ())), preferred_element_type=F32)


def silu(x):
    return x * (1.0 / (1.0 + jnp.exp(-x)))


def fetch(pairs, sems):
    copies = [pltpu.make_async_copy(a, b, sems.at[i]) for i, (a, b) in enumerate(pairs)]
    for copy in copies:
        copy.start()
    return copies


def sort_kernel(tokens_ref, slot_ref, out_ref, held_ref, row_ref, sems):
    for copy in fetch(((tokens_ref, held_ref), (slot_ref, row_ref)), sems):
        copy.wait()
    place = lax.broadcasted_iota(jnp.int32, (SLOTS, SLOTS), 0) == row_ref[...]
    rows = jnp.dot(
        place.astype(F32).astype(BF16), held_ref[...], preferred_element_type=F32
    ).astype(BF16)
    for i in range(32):
        out_ref[i] = rows


def slice_rows(own_ref, other_ref, gain_ref, where_ref):
    group, first = where_ref[0], where_ref[1] == 0
    pieces = []
    for pair in range(4):
        own = own_ref[:, pair].reshape(8 * SLOTS, CHUNK).astype(F32)
        other = other_ref[:, pair].reshape(8 * SLOTS, CHUNK).astype(F32)
        pieces += [jnp.where(first, own, other), jnp.where(first, other, own)]
    rows = jnp.concatenate(pieces, axis=1)
    scaled = [
        (rows[:, 128 * j : 128 * j + 128] * gain_ref[pl.ds(6 * group + j, 1), :]).astype(BF16)
        for j in range(6)
    ]
    return jnp.concatenate(scaled, axis=1), jnp.sum(rows * rows, axis=1, keepdims=True)


def stats_lanes(total, lane):
    high = total.astype(BF16).astype(F32)
    at = lax.broadcasted_iota(jnp.int32, (total.shape[0], 128), 1)
    return jnp.where(at == lane, high, jnp.where(at == lane + 1, total - high, 0.0))


def qkv_kernel(
    own_ref, other_ref, q_ref, k_ref, v_ref, gain_ref, target_ref, where_ref, out_ref, scale_ref, held_ref, sems
):
    pairs = [(ref, held_ref.at[i]) for i, ref in enumerate((q_ref, k_ref, v_ref))]
    gain, *copies = fetch([(gain_ref, scale_ref), *pairs], sems)
    gain.wait()
    rows, total = slice_rows(own_ref, other_ref, scale_ref, where_ref)
    parts = []
    for i, copy in enumerate(copies):
        copy.wait()
        parts.append(jnp.dot(rows, held_ref[i], preferred_element_type=F32))
    pick = lax.broadcasted_iota(jnp.int32, (MIG, SLOTS), 1) == target_ref[...]
    pick = pick.astype(F32).astype(BF16)
    for i, part in enumerate((*parts, stats_lanes(total, 0))):
        part = part.astype(BF16)
        lanes = slice(128 * i, 128 * i + 128)
        out_ref[:, :SLOTS, lanes] = part.reshape(8, SLOTS, 128)
        moved = jnp.dot(pick, part[7 * SLOTS :], preferred_element_type=F32).astype(BF16)
        for d in range(8):
            out_ref[d, SLOTS:, lanes] = moved


def attention_kernel(got_ref, states_ref, source_ref, decay_ref, migration_ref, where_ref, out_ref, o_ref):
    total = got_ref[0].astype(F32)
    for i in range(1, 8):
        total += got_ref[i].astype(F32)
    squares = total[:, 384:385] + total[:, 385:386]
    scale = lax.rsqrt(squares * (1.0 / D) + EPS)
    q, k, v = (silu(scale * total[:, 128 * i : 128 * i + 128]) for i in range(3))
    rows = SLOTS + MIG
    turned = jnp.concatenate([q, jnp.zeros((128 - rows, 128), F32)], axis=0).T
    for s in range(SLOTS):
        o_ref[s : s + 1, :] = jnp.sum(turned[:, s : s + 1] * states_ref[s], axis=0, keepdims=True)
    for m in range(MIG):
        s = SLOTS + m
        o_ref[s : s + 1, :] = jnp.sum(
            turned[:, s : s + 1] * states_ref[migration_ref[m, 1]], axis=0, keepdims=True
        )
    retain = jnp.exp(-decay_ref[...])
    mixed = retain * o_ref[...] + jnp.sum(q * k, axis=1, keepdims=True) * v
    heads = mixed * lax.rsqrt(jnp.mean(mixed * mixed, axis=1, keepdims=True) + EPS)
    here = source_ref[...] == where_ref[0]
    own = heads[:SLOTS].astype(BF16)
    moved = jnp.where(here, heads[SLOTS:], 0.0).astype(BF16)
    for d in range(8):
        out_ref[d, :SLOTS] = own
        out_ref[d, SLOTS:] = moved


def output_kernel(got_ref, weight_ref, target_ref, where_ref, keep_ref, send_ref):
    core = where_ref[1]
    moved = got_ref[0, SLOTS:].astype(F32)
    for i in range(1, 8):
        moved += got_ref[i, SLOTS:].astype(F32)
    place = lax.broadcasted_iota(jnp.int32, (SLOTS, MIG), 0) == target_ref[...]
    place = place.astype(F32)
    landed = jnp.dot(place.astype(BF16), moved.astype(BF16), preferred_element_type=F32)
    taken = jnp.sum(place, axis=1, keepdims=True) > 0.0
    last = jnp.where(taken, landed, got_ref[7, :SLOTS].astype(F32)).astype(BF16)
    rows = jnp.concatenate([got_ref[:7, :SLOTS].reshape(7 * SLOTS, DH), last], axis=0)
    for pair in range(4):
        for ref, side in ((keep_ref, core), (send_ref, 1 - core)):
            at = pl.multiple_of((2 * pair + side) * CHUNK, 32)
            part = dot_nt(rows, weight_ref[pl.ds(at, CHUNK), :])
            ref[:, pair] = part.reshape(8, SLOTS, CHUNK).astype(ref.dtype)


def resid_kernel(got_ref, tokens_ref, where_ref, spread_ref):
    total = got_ref[0].astype(F32)
    for i in range(1, 32):
        total += got_ref[i].astype(F32)
    tokens = tokens_ref[where_ref[3], where_ref[4]]
    resid = (tokens.astype(F32) + total).astype(BF16)
    for i in range(32):
        spread_ref[i] = resid


def gate_kernel(own_ref, other_ref, gate_ref, up_ref, router_ref, gain_ref, where_ref, out_ref):
    rows, total = slice_rows(own_ref, other_ref, gain_ref, where_ref)
    gate = dot_nt(rows, gate_ref[:256])
    up = dot_nt(rows, up_ref[:256])
    at = pl.multiple_of(where_ref[0] * SLICE, SLICE)
    router = router_ref[:, pl.ds(at, SLICE)]
    rest = jnp.concatenate([gate_ref[256:], up_ref[256:], router, jnp.zeros_like(router)], axis=0)
    tail = dot_nt(rows, rest) + stats_lanes(total, 96)
    out_ref[:, :, :256] = gate.astype(BF16).reshape(8, SLOTS, 256)
    out_ref[:, :, 256:512] = up.astype(BF16).reshape(8, SLOTS, 256)
    out_ref[:, :, 512:640] = tail.astype(BF16).reshape(8, SLOTS, 128)
    for d in range(8):
        out_ref[d, :, 640:736] = own_ref[d, where_ref[4]]
        out_ref[d, :, 736:] = jnp.zeros((SLOTS, 32), BF16)


def hidden_kernel(got_ref, ids_ref, slot_row_ref, where_ref, out_ref, resid_ref):
    expert = where_ref[2]
    resid_ref[...] = got_ref[where_ref[3], :, 640:736]
    total = got_ref[0].astype(F32)
    for i in range(1, 8):
        total += got_ref[i].astype(F32)
    tail = total[:, 512:640]
    scale = lax.rsqrt((tail[:, 96:97] + tail[:, 97:98]) * (1.0 / D) + EPS)
    main = silu(scale * total[:, :256]) * (scale * total[:, 256:512])
    rest = silu(scale * tail[:, :32]) * (scale * tail[:, 32:64])
    logits = scale * tail[:, 64:96]
    place = lax.broadcasted_iota(jnp.int32, (SLOTS, SLOTS), 0) == slot_row_ref[...]
    ids = jnp.dot(
        place.astype(F32).astype(BF16), ids_ref[...].astype(F32).astype(BF16), preferred_element_type=F32
    )
    ids = (ids + 0.5).astype(jnp.int32)
    at = lax.broadcasted_iota(jnp.int32, (SLOTS, 32), 1)
    lifted = []
    for i in range(2):
        chosen = jnp.sum(jnp.where(at == ids[:, i : i + 1], logits, 0.0), axis=1, keepdims=True)
        lifted.append(1.0 / (1.0 + jnp.exp(-chosen)))
    mine = jnp.where(ids[:, 0:1] == expert, lifted[0], 0.0)
    mine += jnp.where(ids[:, 1:2] == expert, lifted[1], 0.0)
    share = mine / (lifted[0] + lifted[1])
    main, rest = (main * share).astype(BF16), (rest * share).astype(BF16)
    for d in range(8):
        out_ref[d, :, :256] = main
        out_ref[d, :, 256:] = rest


def down_kernel(got_ref, down_ref, where_ref, keep_ref, send_ref):
    first = where_ref[1] == 0
    part = jnp.dot(
        got_ref[...].reshape(8 * SLOTS, UNITS), down_ref[...], preferred_element_type=F32
    )
    for pair in range(4):
        even = part[:, 192 * pair : 192 * pair + 96]
        odd = part[:, 192 * pair + 96 : 192 * pair + 192]
        keep_ref[:, pair] = jnp.where(first, even, odd).reshape(8, SLOTS, CHUNK)
        send_ref[:, pair] = jnp.where(first, odd, even).astype(BF16).reshape(8, SLOTS, CHUNK)


def final_kernel(got_ref, resid_ref, slot_ref, out_ref):
    total = got_ref[0].astype(F32)
    for i in range(1, 32):
        total += got_ref[i].astype(F32)
    out = (resid_ref[...].astype(F32) + total).astype(BF16)
    place = lax.broadcasted_iota(jnp.int32, (SLOTS, SLOTS), 1) == slot_ref[...]
    out_ref[...] = jnp.dot(
        place.astype(F32).astype(BF16), out, preferred_element_type=F32
    ).astype(BF16)


def in_hbm(x):
    return pltpu.with_memory_space_constraint(x, pltpu.HBM)


def exchange(x, axes):
    return lax.all_to_all(x, axes, 0, 0)


def shards(
    tokens,
    query_weight,
    key_weight,
    value_weight,
    output_weight,
    gate_weight,
    up_weight,
    down_weight,
    router_weight,
    attn_gain,
    expert_gain,
    decay_rate,
    states,
    expert_ids,
    row_slot,
    migration,
):
    group = lax.axis_index(GRP).astype(jnp.int32)
    core = lax.axis_index("c").astype(jnp.int32)
    device = lax.axis_index(EPA).astype(jnp.int32)
    expert = device * UNITS // FF
    where = jnp.stack([group, core, expert, device // 8, device % 8 // 2])
    slot_row, slot_column = row_slot[None, :], row_slot[:, None]

    attn_gain, expert_gain = attn_gain.reshape(48, 128), expert_gain.reshape(48, 128)

    def merge(keep, send):
        return (keep + lax.ppermute(send, "c", CORES).astype(F32)).astype(BF16)

    spread = pl.pallas_call(
        sort_kernel,
        out_shape=shape((32, SLOTS, CHUNK), BF16),
        in_specs=[HBM, HBM],
        out_specs=VMEM,
        scratch_shapes=[
            pltpu.VMEM((SLOTS, CHUNK), BF16),
            pltpu.VMEM((1, SLOTS), jnp.int32),
            pltpu.SemaphoreType.DMA((2,)),
        ],
        name="sorted_rows",
    )(in_hbm(tokens), in_hbm(slot_row))
    own = exchange(exchange(spread, CHIPS).reshape(8, 4, SLOTS, CHUNK), GRP)
    rows_own, other = own, lax.ppermute(own, "c", CORES)
    parts = pl.pallas_call(
        qkv_kernel,
        out_shape=shape((8, SLOTS + MIG, 512), BF16),
        in_specs=[VMEM, VMEM, HBM, HBM, HBM, HBM, VMEM, SMEM],
        out_specs=VMEM,
        scratch_shapes=[
            pltpu.VMEM((48, 128), F32),
            pltpu.VMEM((3, SLICE, DH), BF16),
            pltpu.SemaphoreType.DMA((4,)),
        ],
        compiler_params=pltpu.CompilerParams(vmem_limit_bytes=16 << 20),
        name="qkv_parts",
    )(
        own,
        other,
        in_hbm(query_weight),
        in_hbm(key_weight),
        in_hbm(value_weight),
        in_hbm(attn_gain),
        migration[:, 2:3],
        where,
    )
    parts = exchange(parts, GRP)
    heads = pl.pallas_call(
        attention_kernel,
        out_shape=shape((8, SLOTS + MIG, DH), BF16),
        in_specs=[VMEM, VMEM, VMEM, VMEM, SMEM, SMEM],
        out_specs=VMEM,
        scratch_shapes=[pltpu.VMEM((SLOTS + MIG, DH), F32)],
        compiler_params=pltpu.CompilerParams(vmem_limit_bytes=16 << 20),
        name="attention",
    )(parts, states[:, 0], migration[:, 0:1], decay_rate[None], migration, where)
    heads = exchange(heads, GRP)
    keep, send = call(
        output_kernel,
        (shape((8, 4, SLOTS, CHUNK), F32), shape((8, 4, SLOTS, CHUNK), BF16)),
        (heads, output_weight, migration[:, 2][None, :], where),
        "output_parts",
        smem=(3,),
    )
    spread = call(
        resid_kernel,
        shape((32, SLOTS, CHUNK), BF16),
        (
            exchange(merge(keep, send).reshape(32, SLOTS, CHUNK), CHIPS),
            rows_own,
            where,
        ),
        "resid",
        smem=(2,),
    )
    own = exchange(spread, CHIPS).reshape(8, 4, SLOTS, CHUNK)
    other = lax.ppermute(own, "c", CORES)
    parts = call(
        gate_kernel,
        shape((8, SLOTS, 768), BF16),
        (own, other, gate_weight.T, up_weight.T, router_weight.T, expert_gain, where),
        "gate_parts",
        smem=(6,),
    )
    parts = exchange(parts, GRP)
    hidden, resid = call(
        hidden_kernel,
        (shape((8, SLOTS, UNITS), BF16), shape((SLOTS, CHUNK), BF16)),
        (parts, expert_ids, slot_row, where),
        "hidden",
        smem=(3,),
    )
    hidden = exchange(hidden, GRP)
    keep, send = call(
        down_kernel,
        (shape((8, 4, SLOTS, CHUNK), F32), shape((8, 4, SLOTS, CHUNK), BF16)),
        (hidden, down_weight.T, where),
        "down_parts",
        smem=(2,),
    )
    parts = exchange(merge(keep, send), GRP)
    parts = exchange(parts.reshape(32, SLOTS, CHUNK), CHIPS)
    return call(
        final_kernel,
        shape((SLOTS, CHUNK), BF16),
        (parts, resid, slot_column),
        "layer_out",
    )


def solution(mesh):
    fine = jax.sharding.Mesh(
        mesh.devices.reshape(2, 4, 4, 2, 4, 2), ("yl", "x", "yh", "zh", "zl", "c")
    )
    both = P(GRP, EPA)
    placed = (both,) * 8 + (
        P(),
        P(),
        P(),
        P(EPA),
        P(GRP, EPA, None, None),
        P(GRP, None),
        P(GRP),
        P(),
    )
    return jax.shard_map(shards, mesh=fine, in_specs=placed, out_specs=both, check_vma=False)
```

```python
import jax
import jax.numpy as jnp
from jax import lax
from jax.experimental import pallas as pl
from jax.experimental.pallas import tpu as pltpu
from jax.sharding import PartitionSpec as P

BF16, F32 = jnp.bfloat16, jnp.float32
GRP = ("yl", "x")
EPA = ("yh", "zh", "zl", "c")
CHIPS = ("yh", "zh", "zl")
CORES = [(0, 1), (1, 0)]
D, FF, DH = 6144, 9216, 128
EPS = 1e-6
PACK = (24, 128)
CHUNK, HALF, SLICE, SLOTS, MIG, UNITS = 96, 384, 768, 32, 16, 288
VMEM = pl.BlockSpec(memory_space=pltpu.VMEM)
HBM = pl.BlockSpec(memory_space=pltpu.HBM)
SMEM = pl.BlockSpec(memory_space=pltpu.SMEM)


def call(kernel, outs, ins, name, smem=(), limit=16 << 20):
    specs = [SMEM if i in smem else VMEM for i in range(len(ins))]
    return pl.pallas_call(
        kernel,
        out_shape=outs,
        in_specs=specs,
        out_specs=jax.tree.map(lambda _: VMEM, outs),
        compiler_params=pltpu.CompilerParams(vmem_limit_bytes=limit),
        name=name,
    )(*ins)


def shape(dims, dtype):
    return jax.ShapeDtypeStruct(dims, dtype)


def dot_nt(left, right):
    return lax.dot_general(left, right, (((1,), (1,)), ((), ())), preferred_element_type=F32)


def silu(x):
    return x * (1.0 / (1.0 + jnp.exp(-x)))


def packed(rows):
    last = rows[..., 24:, :]
    beside = jnp.concatenate([last[..., 32 * i : 32 * i + 32] for i in range(3)], axis=-2)
    return jnp.concatenate([rows[..., :24, :], beside], axis=-1)


def unpacked(rows):
    beside = rows[..., CHUNK:]
    last = jnp.concatenate([beside[..., 8 * i : 8 * i + 8, :] for i in range(3)], axis=-1)
    return jnp.concatenate([rows[..., :CHUNK], last], axis=-2)


def fetch(pairs, sems):
    copies = [pltpu.make_async_copy(a, b, sems.at[i]) for i, (a, b) in enumerate(pairs)]
    for copy in copies:
        copy.start()
    return copies


def sort_kernel(tokens_ref, slot_ref, out_ref, held_ref, row_ref, sems):
    for copy in fetch(((tokens_ref, held_ref), (slot_ref, row_ref)), sems):
        copy.wait()
    place = lax.broadcasted_iota(jnp.int32, (SLOTS, SLOTS), 0) == row_ref[...]
    rows = packed(
        jnp.dot(place.astype(F32).astype(BF16), held_ref[...], preferred_element_type=F32)
    ).astype(BF16)
    for i in range(32):
        out_ref[i] = rows


def chunk_rows(own_ref, other_ref, first):
    pieces = []
    for pair in range(4):
        own = unpacked(own_ref[:, pair].astype(F32)).reshape(8 * SLOTS, CHUNK)
        other = unpacked(other_ref[:, pair].astype(F32)).reshape(8 * SLOTS, CHUNK)
        pieces += [jnp.where(first, own, other), jnp.where(first, other, own)]
    return jnp.concatenate(pieces, axis=1)


def scaled_rows(rows, gain_ref, group):
    scaled = [
        (rows[:, 128 * j : 128 * j + 128] * gain_ref[pl.ds(6 * group + j, 1), :]).astype(BF16)
        for j in range(6)
    ]
    return jnp.concatenate(scaled, axis=1), jnp.sum(rows * rows, axis=1, keepdims=True)


def stats_lanes(total, lane):
    high = total.astype(BF16).astype(F32)
    at = lax.broadcasted_iota(jnp.int32, (total.shape[0], 128), 1)
    return jnp.where(at == lane, high, jnp.where(at == lane + 1, total - high, 0.0))


def qkv_kernel(
    own_ref, other_ref, q_ref, k_ref, v_ref, gain_ref, target_ref, where_ref, out_ref, tokens_ref, scale_ref, held_ref, half_ref, sems
):
    pairs = [(ref, held_ref.at[:, pl.ds(128 * i, 128)]) for i, ref in enumerate((q_ref, k_ref, v_ref))]
    gain, *copies = fetch([(gain_ref, scale_ref), *pairs], sems)
    first = where_ref[1] == 0
    rows = chunk_rows(own_ref, other_ref, first)
    half_ref[...] = jnp.where(first, rows[:, :HALF], rows[:, HALF:])
    tokens_ref[...] = half_ref[pl.ds(pl.multiple_of(8 * where_ref[4], 8), 8), :]
    gain.wait()
    rows, total = scaled_rows(rows, scale_ref, where_ref[0])
    for copy in copies:
        copy.wait()
    parts = jnp.dot(rows, held_ref[...], preferred_element_type=F32)
    parts = jnp.concatenate([parts, stats_lanes(total, 0)], axis=1).astype(BF16)
    pick = lax.broadcasted_iota(jnp.int32, (MIG, SLOTS), 1) == target_ref[...]
    pick = pick.astype(F32).astype(BF16)
    moved = jnp.dot(pick, parts[7 * SLOTS :], preferred_element_type=F32).astype(BF16)
    out_ref[:, :SLOTS] = parts.reshape(8, SLOTS, 512)
    for d in range(8):
        out_ref[d, SLOTS:] = moved


def attention_kernel(got_ref, states_ref, source_ref, decay_ref, migration_ref, where_ref, out_ref, o_ref):
    total = got_ref[0].astype(F32)
    for i in range(1, 8):
        total += got_ref[i].astype(F32)
    squares = total[:, 384:385] + total[:, 385:386]
    scale = lax.rsqrt(squares * (1.0 / D) + EPS)
    q, k, v = (silu(scale * total[:, 128 * i : 128 * i + 128]) for i in range(3))
    rows = SLOTS + MIG
    turned = jnp.concatenate([q, jnp.zeros((128 - rows, 128), F32)], axis=0).T
    for s in range(SLOTS):
        o_ref[s : s + 1, :] = jnp.sum(turned[:, s : s + 1] * states_ref[s], axis=0, keepdims=True)
    for m in range(MIG):
        s = SLOTS + m
        o_ref[s : s + 1, :] = jnp.sum(
            turned[:, s : s + 1] * states_ref[migration_ref[m, 1]], axis=0, keepdims=True
        )
    retain = jnp.exp(-decay_ref[...])
    mixed = retain * o_ref[...] + jnp.sum(q * k, axis=1, keepdims=True) * v
    heads = mixed * lax.rsqrt(jnp.mean(mixed * mixed, axis=1, keepdims=True) + EPS)
    here = source_ref[...] == where_ref[0]
    own = heads[:SLOTS].astype(BF16)
    moved = jnp.where(here, heads[SLOTS:], 0.0).astype(BF16)
    for d in range(8):
        out_ref[d, :SLOTS] = own
        out_ref[d, SLOTS:] = moved


def output_kernel(got_ref, weight_ref, target_ref, where_ref, keep_ref, send_ref):
    first = where_ref[1] == 0
    moved = got_ref[0, SLOTS:].astype(F32)
    for i in range(1, 8):
        moved += got_ref[i, SLOTS:].astype(F32)
    place = lax.broadcasted_iota(jnp.int32, (SLOTS, MIG), 0) == target_ref[...]
    place = place.astype(F32)
    landed = jnp.dot(place.astype(BF16), moved.astype(BF16), preferred_element_type=F32)
    taken = jnp.sum(place, axis=1, keepdims=True) > 0.0
    last = jnp.where(taken, landed, got_ref[7, :SLOTS].astype(F32)).astype(BF16)
    rows = jnp.concatenate([got_ref[:7, :SLOTS].reshape(7 * SLOTS, DH), last], axis=0)
    part = dot_nt(rows, weight_ref[...])
    low, high = part[:, :HALF], part[:, HALF:]
    keep_ref[...] = jnp.where(first, low, high).reshape(32, 8, HALF)
    send_ref[...] = jnp.where(first, high, low).reshape(32, 8, HALF).astype(BF16)


def resid_kernel(got_ref, tokens_ref, spread_ref):
    total = got_ref[0].astype(F32)
    for i in range(1, 32):
        total += got_ref[i].astype(F32)
    resid = (tokens_ref[...] + total).astype(BF16)
    for i in range(32):
        spread_ref[i] = resid


def gate_kernel(
    own_ref, other_ref, gate_ref, up_ref, router_ref, gain_ref, where_ref, out_ref, blocks_ref
):
    first = where_ref[1] == 0
    own = own_ref[...].astype(F32).reshape(8 * SLOTS, HALF)
    other = other_ref[...].astype(F32).reshape(8 * SLOTS, HALF)
    rows = jnp.concatenate([jnp.where(first, own, other), jnp.where(first, other, own)], axis=1)
    start = lax.broadcasted_iota(jnp.int32, (SLICE, CHUNK), 0) - CHUNK * where_ref[5]
    pick = (start == lax.broadcasted_iota(jnp.int32, (SLICE, CHUNK), 1)).astype(F32).astype(BF16)
    blocks = jnp.dot(rows.astype(BF16), pick, preferred_element_type=F32)
    blocks_ref[...] = blocks.astype(BF16).reshape(8, SLOTS, CHUNK)
    rows, total = scaled_rows(rows, gain_ref, where_ref[0])
    gate = dot_nt(rows, gate_ref[:256])
    up = dot_nt(rows, up_ref[:256])
    at = pl.multiple_of(where_ref[0] * SLICE, SLICE)
    router = router_ref[:, pl.ds(at, SLICE)]
    rest = jnp.concatenate([gate_ref[256:], up_ref[256:], router, jnp.zeros_like(router)], axis=0)
    tail = dot_nt(rows, rest) + stats_lanes(total, 96)
    out_ref[:, :, :256] = gate.astype(BF16).reshape(8, SLOTS, 256)
    out_ref[:, :, 256:512] = up.astype(BF16).reshape(8, SLOTS, 256)
    out_ref[:, :, 512:640] = tail.astype(BF16).reshape(8, SLOTS, 128)


def hidden_kernel(got_ref, blocks_ref, ids_ref, slot_row_ref, where_ref, out_ref):
    expert = where_ref[2]
    total = got_ref[0].astype(F32)
    for i in range(1, 8):
        total += got_ref[i].astype(F32)
    tail = total[:, 512:640]
    scale = lax.rsqrt((tail[:, 96:97] + tail[:, 97:98]) * (1.0 / D) + EPS)
    main = silu(scale * total[:, :256]) * (scale * total[:, 256:512])
    rest = silu(scale * tail[:, :32]) * (scale * tail[:, 32:64])
    logits = scale * tail[:, 64:96]
    place = lax.broadcasted_iota(jnp.int32, (SLOTS, SLOTS), 0) == slot_row_ref[...]
    ids = jnp.dot(
        place.astype(F32).astype(BF16), ids_ref[...].astype(F32).astype(BF16), preferred_element_type=F32
    )
    ids = (ids + 0.5).astype(jnp.int32)
    at = lax.broadcasted_iota(jnp.int32, (SLOTS, 32), 1)
    lifted = []
    for i in range(2):
        chosen = jnp.sum(jnp.where(at == ids[:, i : i + 1], logits, 0.0), axis=1, keepdims=True)
        lifted.append(1.0 / (1.0 + jnp.exp(-chosen)))
    mine = jnp.where(ids[:, 0:1] == expert, lifted[0], 0.0)
    mine += jnp.where(ids[:, 1:2] == expert, lifted[1], 0.0)
    share = mine / (lifted[0] + lifted[1])
    main, rest = (main * share).astype(BF16), rest * share
    for d in range(8):
        out_ref[d, :, :256] = main
        out_ref[d, :, 256:] = jnp.concatenate([rest, blocks_ref[d].astype(F32)], axis=1).astype(BF16)


def down_kernel(got_ref, down_ref, where_ref, keep_ref, send_ref, resid_ref):
    first = where_ref[1] == 0
    part = jnp.dot(
        got_ref[:, :, :UNITS].reshape(8 * SLOTS, UNITS), down_ref[...], preferred_element_type=F32
    )
    resid_ref[...] = got_ref[where_ref[3], :, UNITS:]
    for pair in range(4):
        even = part[:, 192 * pair : 192 * pair + 96]
        odd = part[:, 192 * pair + 96 : 192 * pair + 192]
        keep_ref[:, pair] = packed(jnp.where(first, even, odd).reshape(8, SLOTS, CHUNK))
        sent = packed(jnp.where(first, odd, even).reshape(8, SLOTS, CHUNK))
        send_ref[:, pair] = sent.astype(BF16)


def final_kernel(got_ref, resid_ref, slot_ref, out_ref):
    total = got_ref[0].astype(F32)
    for i in range(1, 32):
        total += got_ref[i].astype(F32)
    out = (resid_ref[...].astype(F32) + unpacked(total)).astype(BF16)
    place = lax.broadcasted_iota(jnp.int32, (SLOTS, SLOTS), 1) == slot_ref[...]
    out_ref[...] = jnp.dot(
        place.astype(F32).astype(BF16), out, preferred_element_type=F32
    ).astype(BF16)


def in_hbm(x):
    return pltpu.with_memory_space_constraint(x, pltpu.HBM)


def exchange(x, axes):
    return lax.all_to_all(x, axes, 0, 0)


def shards(
    tokens,
    query_weight,
    key_weight,
    value_weight,
    output_weight,
    gate_weight,
    up_weight,
    down_weight,
    router_weight,
    attn_gain,
    expert_gain,
    decay_rate,
    states,
    expert_ids,
    row_slot,
    migration,
):
    group = lax.axis_index(GRP).astype(jnp.int32)
    core = lax.axis_index("c").astype(jnp.int32)
    device = lax.axis_index(EPA).astype(jnp.int32)
    expert = device * UNITS // FF
    where = jnp.stack([group, core, expert, device // 8, device // 2, device % 8])
    slot_row, slot_column = row_slot[None, :], row_slot[:, None]

    attn_gain, expert_gain = attn_gain.reshape(48, 128), expert_gain.reshape(48, 128)

    def merge(keep, send):
        return (keep + lax.ppermute(send, "c", CORES).astype(F32)).astype(BF16)

    spread = pl.pallas_call(
        sort_kernel,
        out_shape=shape((32, *PACK), BF16),
        in_specs=[HBM, HBM],
        out_specs=VMEM,
        scratch_shapes=[
            pltpu.VMEM((SLOTS, CHUNK), BF16),
            pltpu.VMEM((1, SLOTS), jnp.int32),
            pltpu.SemaphoreType.DMA((2,)),
        ],
        name="sorted_rows",
    )(in_hbm(tokens), in_hbm(slot_row))
    own = exchange(exchange(spread, CHIPS).reshape(8, 4, *PACK), GRP)
    other = lax.ppermute(own, "c", CORES)
    parts, block = pl.pallas_call(
        qkv_kernel,
        out_shape=(shape((8, SLOTS + MIG, 512), BF16), shape((8, HALF), F32)),
        in_specs=[VMEM, VMEM, HBM, HBM, HBM, HBM, VMEM, SMEM],
        out_specs=(VMEM, VMEM),
        scratch_shapes=[
            pltpu.VMEM((48, 128), F32),
            pltpu.VMEM((SLICE, 3 * DH), BF16),
            pltpu.VMEM((8 * SLOTS, HALF), F32),
            pltpu.SemaphoreType.DMA((4,)),
        ],
        compiler_params=pltpu.CompilerParams(vmem_limit_bytes=16 << 20),
        name="qkv_parts",
    )(
        own,
        other,
        in_hbm(query_weight),
        in_hbm(key_weight),
        in_hbm(value_weight),
        in_hbm(attn_gain),
        migration[:, 2:3],
        where,
    )
    parts = exchange(parts, GRP)
    heads = pl.pallas_call(
        attention_kernel,
        out_shape=shape((8, SLOTS + MIG, DH), BF16),
        in_specs=[VMEM, VMEM, VMEM, VMEM, SMEM, SMEM],
        out_specs=VMEM,
        scratch_shapes=[pltpu.VMEM((SLOTS + MIG, DH), F32)],
        compiler_params=pltpu.CompilerParams(vmem_limit_bytes=16 << 20),
        name="attention",
    )(parts, states[:, 0], migration[:, 0:1], decay_rate[None], migration, where)
    heads = exchange(heads, GRP)
    keep, send = call(
        output_kernel,
        (shape((32, 8, HALF), F32), shape((32, 8, HALF), BF16)),
        (heads, output_weight, migration[:, 2][None, :], where),
        "output_parts",
        smem=(3,),
    )
    spread = call(
        resid_kernel,
        shape((32, 8, HALF), BF16),
        (exchange(merge(keep, send), CHIPS), block),
        "resid",
    )
    own = exchange(spread, CHIPS)
    other = lax.ppermute(own, "c", CORES)
    parts, blocks = call(
        gate_kernel,
        (shape((8, SLOTS, 640), BF16), shape((8, SLOTS, CHUNK), BF16)),
        (own, other, gate_weight.T, up_weight.T, router_weight.T, expert_gain, where),
        "gate_parts",
        smem=(6,),
    )
    parts = exchange(parts, GRP)
    hidden = call(
        hidden_kernel,
        shape((8, SLOTS, UNITS + CHUNK), BF16),
        (parts, blocks, expert_ids, slot_row, where),
        "hidden",
        smem=(4,),
    )
    hidden = exchange(hidden, GRP)
    keep, send, resid = call(
        down_kernel,
        (
            shape((8, 4, *PACK), F32),
            shape((8, 4, *PACK), BF16),
            shape((SLOTS, CHUNK), BF16),
        ),
        (hidden, down_weight.T, where),
        "down_parts",
        smem=(2,),
    )
    parts = exchange(merge(keep, send), GRP)
    parts = exchange(parts.reshape(32, *PACK), CHIPS)
    return call(
        final_kernel,
        shape((SLOTS, CHUNK), BF16),
        (parts, resid, slot_column),
        "layer_out",
    )


def solution(mesh):
    fine = jax.sharding.Mesh(
        mesh.devices.reshape(2, 4, 4, 2, 4, 2), ("yl", "x", "yh", "zh", "zl", "c")
    )
    both = P(GRP, EPA)
    placed = (both,) * 8 + (
        P(),
        P(),
        P(),
        P(EPA),
        P(GRP, EPA, None, None),
        P(GRP, None),
        P(GRP),
        P(),
    )
    return jax.shard_map(shards, mesh=fine, in_specs=placed, out_specs=both, check_vma=False)
```

```python
import jax
import jax.numpy as jnp
from jax import lax
from jax.experimental import pallas as pl
from jax.experimental.pallas import tpu as pltpu
from jax.sharding import PartitionSpec as P

BF16, F32 = jnp.bfloat16, jnp.float32
GRP = ("yl", "x")
EPA = ("yh", "zh", "zl", "c")
CHIPS = ("yh", "zh", "zl")
CORES = [(0, 1), (1, 0)]
D, FF, DH = 6144, 9216, 128
EPS = 1e-6
PACK = (24, 128)
CHUNK, HALF, SLICE, SLOTS, MIG, UNITS = 96, 384, 768, 32, 16, 288
VMEM = pl.BlockSpec(memory_space=pltpu.VMEM)
HBM = pl.BlockSpec(memory_space=pltpu.HBM)
SMEM = pl.BlockSpec(memory_space=pltpu.SMEM)


def call(kernel, outs, ins, name, smem=(), limit=16 << 20):
    specs = [SMEM if i in smem else VMEM for i in range(len(ins))]
    return pl.pallas_call(
        kernel,
        out_shape=outs,
        in_specs=specs,
        out_specs=jax.tree.map(lambda _: VMEM, outs),
        compiler_params=pltpu.CompilerParams(vmem_limit_bytes=limit),
        name=name,
    )(*ins)


def index_of(axes):
    return lax.axis_index(axes).astype(jnp.int32)


def shape(dims, dtype):
    return jax.ShapeDtypeStruct(dims, dtype)


def dot_nt(left, right):
    return lax.dot_general(left, right, (((1,), (1,)), ((), ())), preferred_element_type=F32)


def silu(x):
    return x * (1.0 / (1.0 + jnp.exp(-x)))


def packed(rows):
    last = rows[..., 24:, :]
    beside = jnp.concatenate([last[..., 32 * i : 32 * i + 32] for i in range(3)], axis=-2)
    return jnp.concatenate([rows[..., :24, :], beside], axis=-1)


def unpacked(rows):
    beside = rows[..., CHUNK:]
    last = jnp.concatenate([beside[..., 8 * i : 8 * i + 8, :] for i in range(3)], axis=-1)
    return jnp.concatenate([rows[..., :CHUNK], last], axis=-2)


def fetch(pairs, sems):
    copies = [pltpu.make_async_copy(a, b, sems.at[i]) for i, (a, b) in enumerate(pairs)]
    for copy in copies:
        copy.start()
    return copies


def sort_kernel(tokens_ref, slot_ref, out_ref, held_ref, row_ref, sems):
    for copy in fetch(((tokens_ref, held_ref), (slot_ref, row_ref)), sems):
        copy.wait()
    place = lax.broadcasted_iota(jnp.int32, (SLOTS, SLOTS), 0) == row_ref[...]
    rows = packed(
        jnp.dot(place.astype(F32).astype(BF16), held_ref[...], preferred_element_type=F32)
    ).astype(BF16)
    for i in range(32):
        out_ref[i] = rows


def chunk_rows(own_ref, other_ref, first):
    pieces = []
    for pair in range(4):
        own = unpacked(own_ref[:, pair].astype(F32)).reshape(8 * SLOTS, CHUNK)
        other = unpacked(other_ref[:, pair].astype(F32)).reshape(8 * SLOTS, CHUNK)
        pieces += [jnp.where(first, own, other), jnp.where(first, other, own)]
    return jnp.concatenate(pieces, axis=1)


def scaled_rows(rows, gain_ref, group):
    scaled = [
        (rows[:, 128 * j : 128 * j + 128] * gain_ref[pl.ds(6 * group + j, 1), :]).astype(BF16)
        for j in range(6)
    ]
    return jnp.concatenate(scaled, axis=1), jnp.sum(rows * rows, axis=1, keepdims=True)


def stats_lanes(total, lane):
    high = total.astype(BF16).astype(F32)
    at = lax.broadcasted_iota(jnp.int32, (total.shape[0], 128), 1)
    return jnp.where(at == lane, high, jnp.where(at == lane + 1, total - high, 0.0))


def targets(migration_ref):
    row = lax.broadcasted_iota(jnp.int32, (MIG, SLOTS), 0)
    slot = lax.broadcasted_iota(jnp.int32, (MIG, SLOTS), 1)
    found = jnp.zeros((MIG, SLOTS), F32)
    for m in range(MIG):
        found = jnp.where((row == m) & (slot == migration_ref[2, m]), 1.0, found)
    return found


def qkv_kernel(
    own_ref, other_ref, q_ref, k_ref, v_ref, gain_ref, listed_ref, out_ref, tokens_ref,
    scale_ref, held_ref, half_ref, migration_ref, sems
):
    pairs = [(ref, held_ref.at[:, pl.ds(128 * i, 128)]) for i, ref in enumerate((q_ref, k_ref, v_ref))]
    gain, *copies = fetch([(gain_ref, scale_ref), *pairs, (listed_ref, migration_ref)], sems)
    first = index_of("c") == 0
    rows = chunk_rows(own_ref, other_ref, first)
    half_ref[...] = jnp.where(first, rows[:, :HALF], rows[:, HALF:])
    tokens_ref[...] = half_ref[pl.ds(pl.multiple_of(8 * index_of(CHIPS), 8), 8), :]
    gain.wait()
    rows, total = scaled_rows(rows, scale_ref, index_of(GRP))
    for copy in copies:
        copy.wait()
    parts = jnp.dot(rows, held_ref[...], preferred_element_type=F32)
    parts = jnp.concatenate([parts, stats_lanes(total, 0)], axis=1).astype(BF16)
    pick = targets(migration_ref).astype(BF16)
    moved = jnp.dot(pick, parts[7 * SLOTS :], preferred_element_type=F32).astype(BF16)
    out_ref[:, :SLOTS] = parts.reshape(8, SLOTS, 512)
    for d in range(8):
        out_ref[d, SLOTS:] = moved


def attention_kernel(
    got_ref, states_ref, decay_ref, listed_ref, out_ref, place_ref, o_ref, migration_ref, sems
):
    (copy,) = fetch([(listed_ref, migration_ref)], sems)
    total = got_ref[0].astype(F32)
    for i in range(1, 8):
        total += got_ref[i].astype(F32)
    squares = total[:, 384:385] + total[:, 385:386]
    scale = lax.rsqrt(squares * (1.0 / D) + EPS)
    q, k, v = (silu(scale * total[:, 128 * i : 128 * i + 128]) for i in range(3))
    rows = SLOTS + MIG
    turned = jnp.concatenate([q, jnp.zeros((128 - rows, 128), F32)], axis=0).T
    for s in range(SLOTS):
        o_ref[s : s + 1, :] = jnp.sum(turned[:, s : s + 1] * states_ref[s], axis=0, keepdims=True)
    copy.wait()
    place_ref[...] = targets(migration_ref).T
    for m in range(MIG):
        s = SLOTS + m
        o_ref[s : s + 1, :] = jnp.sum(
            turned[:, s : s + 1] * states_ref[migration_ref[1, m]], axis=0, keepdims=True
        )
    retain = jnp.exp(jnp.full((1, DH), -decay_ref[0], F32))
    mixed = retain * o_ref[...] + jnp.sum(q * k, axis=1, keepdims=True) * v
    heads = mixed * lax.rsqrt(jnp.mean(mixed * mixed, axis=1, keepdims=True) + EPS)
    own, moved = heads[:SLOTS].astype(BF16), heads[SLOTS:]
    row, group = lax.broadcasted_iota(jnp.int32, (MIG, DH), 0), index_of(GRP)
    for m in range(MIG):
        moved = jnp.where((row == m) & (migration_ref[0, m] != group), 0.0, moved)
    moved = moved.astype(BF16)
    for d in range(8):
        out_ref[d, :SLOTS] = own
        out_ref[d, SLOTS:] = moved


def output_kernel(got_ref, weight_ref, place_ref, keep_ref, send_ref):
    first = index_of("c") == 0
    moved = got_ref[0, SLOTS:].astype(F32)
    for i in range(1, 8):
        moved += got_ref[i, SLOTS:].astype(F32)
    place = place_ref[...]
    landed = jnp.dot(place.astype(BF16), moved.astype(BF16), preferred_element_type=F32)
    taken = jnp.sum(place, axis=1, keepdims=True) > 0.0
    last = jnp.where(taken, landed, got_ref[7, :SLOTS].astype(F32)).astype(BF16)
    rows = jnp.concatenate([got_ref[:7, :SLOTS].reshape(7 * SLOTS, DH), last], axis=0)
    part = dot_nt(rows, weight_ref[...])
    low, high = part[:, :HALF], part[:, HALF:]
    keep_ref[...] = jnp.where(first, low, high).reshape(32, 8, HALF)
    send_ref[...] = jnp.where(first, high, low).reshape(32, 8, HALF).astype(BF16)


def resid_kernel(got_ref, tokens_ref, spread_ref):
    total = got_ref[0].astype(F32)
    for i in range(1, 32):
        total += got_ref[i].astype(F32)
    resid = (tokens_ref[...] + total).astype(BF16)
    for i in range(32):
        spread_ref[i] = resid


def gate_kernel(
    own_ref, other_ref, gate_ref, up_ref, router_ref, gain_ref, out_ref, blocks_ref
):
    first = index_of("c") == 0
    own = own_ref[...].astype(F32).reshape(8 * SLOTS, HALF)
    other = other_ref[...].astype(F32).reshape(8 * SLOTS, HALF)
    rows = jnp.concatenate([jnp.where(first, own, other), jnp.where(first, other, own)], axis=1)
    start = lax.broadcasted_iota(jnp.int32, (SLICE, CHUNK), 0) - CHUNK * index_of(("zl", "c"))
    pick = (start == lax.broadcasted_iota(jnp.int32, (SLICE, CHUNK), 1)).astype(F32).astype(BF16)
    blocks = jnp.dot(rows.astype(BF16), pick, preferred_element_type=F32)
    blocks_ref[...] = blocks.astype(BF16).reshape(8, SLOTS, CHUNK)
    rows, total = scaled_rows(rows, gain_ref, index_of(GRP))
    gate = dot_nt(rows, gate_ref[:256])
    up = dot_nt(rows, up_ref[:256])
    at = pl.multiple_of(index_of(GRP) * SLICE, SLICE)
    router = router_ref[:, pl.ds(at, SLICE)]
    rest = jnp.concatenate([gate_ref[256:], up_ref[256:], router, jnp.zeros_like(router)], axis=0)
    tail = dot_nt(rows, rest) + stats_lanes(total, 96)
    out_ref[:, :, :256] = gate.astype(BF16).reshape(8, SLOTS, 256)
    out_ref[:, :, 256:512] = up.astype(BF16).reshape(8, SLOTS, 256)
    out_ref[:, :, 512:640] = tail.astype(BF16).reshape(8, SLOTS, 128)


def hidden_kernel(got_ref, blocks_ref, ids_ref, slot_row_ref, out_ref):
    expert = index_of(EPA) * UNITS // FF
    total = got_ref[0].astype(F32)
    for i in range(1, 8):
        total += got_ref[i].astype(F32)
    tail = total[:, 512:640]
    scale = lax.rsqrt((tail[:, 96:97] + tail[:, 97:98]) * (1.0 / D) + EPS)
    main = silu(scale * total[:, :256]) * (scale * total[:, 256:512])
    rest = silu(scale * tail[:, :32]) * (scale * tail[:, 32:64])
    logits = scale * tail[:, 64:96]
    place = lax.broadcasted_iota(jnp.int32, (SLOTS, SLOTS), 0) == slot_row_ref[...]
    ids = dot_nt(place.astype(F32).astype(BF16), ids_ref[...].astype(F32).astype(BF16))
    ids = (ids + 0.5).astype(jnp.int32)
    at = lax.broadcasted_iota(jnp.int32, (SLOTS, 32), 1)
    lifted = []
    for i in range(2):
        chosen = jnp.sum(jnp.where(at == ids[:, i : i + 1], logits, 0.0), axis=1, keepdims=True)
        lifted.append(1.0 / (1.0 + jnp.exp(-chosen)))
    mine = jnp.where(ids[:, 0:1] == expert, lifted[0], 0.0)
    mine += jnp.where(ids[:, 1:2] == expert, lifted[1], 0.0)
    share = mine / (lifted[0] + lifted[1])
    main, rest = (main * share).astype(BF16), rest * share
    for d in range(8):
        out_ref[d, :, :256] = main
        out_ref[d, :, 256:] = jnp.concatenate([rest, blocks_ref[d].astype(F32)], axis=1).astype(BF16)


def down_kernel(got_ref, down_ref, keep_ref, send_ref, resid_ref):
    first = index_of("c") == 0
    part = jnp.dot(
        got_ref[:, :, :UNITS].reshape(8 * SLOTS, UNITS), down_ref[...], preferred_element_type=F32
    )
    resid_ref[...] = got_ref[index_of(("yh", "zh")), :, UNITS:]
    for pair in range(4):
        even = part[:, 192 * pair : 192 * pair + 96]
        odd = part[:, 192 * pair + 96 : 192 * pair + 192]
        keep_ref[:, pair] = packed(jnp.where(first, even, odd).reshape(8, SLOTS, CHUNK))
        sent = packed(jnp.where(first, odd, even).reshape(8, SLOTS, CHUNK))
        send_ref[:, pair] = sent.astype(BF16)


def final_kernel(got_ref, resid_ref, slot_ref, out_ref):
    total = got_ref[0].astype(F32)
    for i in range(1, 32):
        total += got_ref[i].astype(F32)
    out = (resid_ref[...].astype(F32) + unpacked(total)).astype(BF16)
    place = lax.broadcasted_iota(jnp.int32, (SLOTS, SLOTS), 0) == slot_ref[...]
    out_ref[...] = lax.dot_general(
        place.astype(F32).astype(BF16), out, (((0,), (0,)), ((), ())), preferred_element_type=F32
    ).astype(BF16)


def in_hbm(x):
    return pltpu.with_memory_space_constraint(x, pltpu.HBM)


def exchange(x, axes):
    return lax.all_to_all(x, axes, 0, 0)


def shards(
    tokens,
    query_weight,
    key_weight,
    value_weight,
    output_weight,
    gate_weight,
    up_weight,
    down_weight,
    router_weight,
    attn_gain,
    expert_gain,
    decay_rate,
    states,
    expert_ids,
    row_slot,
    migration,
):
    slot_row, migration, expert_ids = row_slot[None, :], migration.T, expert_ids.T
    attn_gain, expert_gain = attn_gain.reshape(48, 128), expert_gain.reshape(48, 128)

    def merge(keep, send):
        return (keep + lax.ppermute(send, "c", CORES).astype(F32)).astype(BF16)

    spread = pl.pallas_call(
        sort_kernel,
        out_shape=pltpu.VMEM((32, *PACK), BF16),
        in_specs=[HBM, HBM],
        out_specs=VMEM,
        scratch_shapes=[
            pltpu.VMEM((SLOTS, CHUNK), BF16),
            pltpu.VMEM((1, SLOTS), jnp.int32),
            pltpu.SemaphoreType.DMA((2,)),
        ],
        name="sorted_rows",
    )(in_hbm(tokens), in_hbm(slot_row))
    own = exchange(exchange(spread, CHIPS).reshape(8, 4, *PACK), GRP)
    other = lax.ppermute(own, "c", CORES)
    parts, block = pl.pallas_call(
        qkv_kernel,
        out_shape=(shape((8, SLOTS + MIG, 512), BF16), shape((8, HALF), F32)),
        in_specs=[VMEM, VMEM, HBM, HBM, HBM, HBM, HBM],
        out_specs=(VMEM, VMEM),
        scratch_shapes=[
            pltpu.VMEM((48, 128), F32),
            pltpu.VMEM((SLICE, 3 * DH), BF16),
            pltpu.VMEM((8 * SLOTS, HALF), F32),
            pltpu.SMEM((3, MIG), jnp.int32),
            pltpu.SemaphoreType.DMA((5,)),
        ],
        compiler_params=pltpu.CompilerParams(vmem_limit_bytes=16 << 20),
        name="qkv_parts",
    )(
        own,
        other,
        in_hbm(query_weight),
        in_hbm(key_weight),
        in_hbm(value_weight),
        in_hbm(attn_gain),
        in_hbm(migration),
    )
    parts = exchange(parts, GRP)
    heads, place = pl.pallas_call(
        attention_kernel,
        out_shape=(shape((8, SLOTS + MIG, DH), BF16), shape((SLOTS, MIG), F32)),
        in_specs=[VMEM, VMEM, SMEM, HBM],
        out_specs=(VMEM, VMEM),
        scratch_shapes=[
            pltpu.VMEM((SLOTS + MIG, DH), F32),
            pltpu.SMEM((3, MIG), jnp.int32),
            pltpu.SemaphoreType.DMA((1,)),
        ],
        compiler_params=pltpu.CompilerParams(vmem_limit_bytes=16 << 20),
        name="attention",
    )(parts, states[:, 0], decay_rate, in_hbm(migration))
    heads = exchange(heads, GRP)
    keep, send = call(
        output_kernel,
        (shape((32, 8, HALF), F32), shape((32, 8, HALF), BF16)),
        (heads, output_weight, place),
        "output_parts",
    )
    spread = call(
        resid_kernel,
        shape((32, 8, HALF), BF16),
        (exchange(merge(keep, send), CHIPS), block),
        "resid",
    )
    own = exchange(spread, CHIPS)
    other = lax.ppermute(own, "c", CORES)
    parts, blocks = call(
        gate_kernel,
        (shape((8, SLOTS, 640), BF16), shape((8, SLOTS, CHUNK), BF16)),
        (own, other, gate_weight.T, up_weight.T, router_weight.T, expert_gain),
        "gate_parts",
    )
    parts = exchange(parts, GRP)
    hidden = call(
        hidden_kernel,
        shape((8, SLOTS, UNITS + CHUNK), BF16),
        (parts, blocks, expert_ids, slot_row),
        "hidden",
    )
    hidden = exchange(hidden, GRP)
    keep, send, resid = call(
        down_kernel,
        (
            shape((8, 4, *PACK), F32),
            shape((8, 4, *PACK), BF16),
            shape((SLOTS, CHUNK), BF16),
        ),
        (hidden, down_weight.T),
        "down_parts",
    )
    parts = exchange(merge(keep, send), GRP)
    parts = exchange(parts.reshape(32, *PACK), CHIPS)
    return call(
        final_kernel,
        shape((SLOTS, CHUNK), BF16),
        (parts, resid, slot_row),
        "layer_out",
    )


def solution(mesh):
    fine = jax.sharding.Mesh(
        mesh.devices.reshape(2, 4, 4, 2, 4, 2), ("yl", "x", "yh", "zh", "zl", "c")
    )
    both = P(GRP, EPA)
    placed = (both,) * 8 + (
        P(),
        P(),
        P(),
        P(EPA),
        P(GRP, EPA, None, None),
        P(GRP, None),
        P(GRP),
        P(),
    )
    return jax.shard_map(shards, mesh=fine, in_specs=placed, out_specs=both, check_vma=False)
```

```python
import jax
import jax.numpy as jnp
from jax import lax
from jax.experimental import pallas as pl
from jax.experimental.pallas import tpu as pltpu
from jax.sharding import PartitionSpec as P

BF16, F32 = jnp.bfloat16, jnp.float32
GRP = ("yl", "x")
EPA = ("yh", "zh", "zl", "c")
CHIPS = ("yh", "zh", "zl")
CORES = [(0, 1), (1, 0)]
D, FF, DH = 6144, 9216, 128
EPS = 1e-6
PACK = (24, 128)
CHUNK, HALF, SLICE, SLOTS, MIG, UNITS = 96, 384, 768, 32, 16, 288
VMEM = pl.BlockSpec(memory_space=pltpu.VMEM)
HBM = pl.BlockSpec(memory_space=pltpu.HBM)
SMEM = pl.BlockSpec(memory_space=pltpu.SMEM)


def call(kernel, outs, ins, name, smem=(), limit=16 << 20):
    specs = [SMEM if i in smem else VMEM for i in range(len(ins))]
    return pl.pallas_call(
        kernel,
        out_shape=outs,
        in_specs=specs,
        out_specs=jax.tree.map(lambda _: VMEM, outs),
        compiler_params=pltpu.CompilerParams(vmem_limit_bytes=limit),
        name=name,
    )(*ins)


def index_of(axes):
    return lax.axis_index(axes).astype(jnp.int32)


def shape(dims, dtype):
    return jax.ShapeDtypeStruct(dims, dtype)


def dot_nt(left, right):
    return lax.dot_general(left, right, (((1,), (1,)), ((), ())), preferred_element_type=F32)


def silu(x):
    return x * (1.0 / (1.0 + jnp.exp(-x)))


def packed(rows):
    last = rows[..., 24:, :]
    beside = jnp.concatenate([last[..., 32 * i : 32 * i + 32] for i in range(3)], axis=-2)
    return jnp.concatenate([rows[..., :24, :], beside], axis=-1)


def unpacked(rows):
    beside = rows[..., CHUNK:]
    last = jnp.concatenate([beside[..., 8 * i : 8 * i + 8, :] for i in range(3)], axis=-1)
    return jnp.concatenate([rows[..., :CHUNK], last], axis=-2)


def fetch(pairs, sems):
    copies = [pltpu.make_async_copy(a, b, sems.at[i]) for i, (a, b) in enumerate(pairs)]
    for copy in copies:
        copy.start()
    return copies


def sort_kernel(
    tokens_ref, slot_ref, q_ref, k_ref, v_ref, gain_ref, decay_ref,
    out_ref, weight_ref, scale_ref, retain_ref, held_ref, row_ref, sems,
):
    pairs = [(ref, weight_ref.at[:, pl.ds(128 * i, 128)]) for i, ref in enumerate((q_ref, k_ref, v_ref))]
    tokens, slots, *copies = fetch(
        [(tokens_ref, held_ref), (slot_ref, row_ref), *pairs, (gain_ref, scale_ref)], sems
    )
    retain_ref[...] = jnp.broadcast_to(jnp.exp(-decay_ref[...]), retain_ref.shape)
    tokens.wait()
    slots.wait()
    place = lax.broadcasted_iota(jnp.int32, (SLOTS, SLOTS), 0) == row_ref[...]
    rows = packed(
        jnp.dot(place.astype(F32).astype(BF16), held_ref[...], preferred_element_type=F32)
    ).astype(BF16)
    for i in range(32):
        out_ref[i] = rows
    for copy in copies:
        copy.wait()


def chunk_rows(got_ref):
    return jnp.concatenate(
        [
            unpacked(got_ref[:, core, pair].astype(F32)).reshape(8 * SLOTS, CHUNK)
            for pair in range(4)
            for core in range(2)
        ],
        axis=1,
    )


def scaled_rows(rows, gain_ref, group):
    scaled = [
        (rows[:, 128 * j : 128 * j + 128] * gain_ref[pl.ds(6 * group + j, 1), :]).astype(BF16)
        for j in range(6)
    ]
    return jnp.concatenate(scaled, axis=1), jnp.sum(rows * rows, axis=1, keepdims=True)


def stats_lanes(total, lane):
    high = total.astype(BF16).astype(F32)
    at = lax.broadcasted_iota(jnp.int32, (total.shape[0], 128), 1)
    return jnp.where(at == lane, high, jnp.where(at == lane + 1, total - high, 0.0))


def targets(migration_ref):
    row = lax.broadcasted_iota(jnp.int32, (MIG, SLOTS), 0)
    slot = lax.broadcasted_iota(jnp.int32, (MIG, SLOTS), 1)
    found = jnp.zeros((MIG, SLOTS), F32)
    for m in range(MIG):
        found = jnp.where((row == m) & (slot == migration_ref[2, m]), 1.0, found)
    return found


def qkv_kernel(
    got_ref, weight_ref, scale_ref, listed_ref, out_ref, tokens_ref, half_ref, migration_ref, sems
):
    (copy,) = fetch([(listed_ref, migration_ref)], sems)
    first = index_of("c") == 0
    rows = chunk_rows(got_ref)
    half_ref[...] = jnp.where(first, rows[:, :HALF], rows[:, HALF:])
    tokens_ref[...] = half_ref[pl.ds(pl.multiple_of(8 * index_of(CHIPS), 8), 8), :]
    rows, total = scaled_rows(rows, scale_ref, index_of(GRP))
    parts = jnp.dot(rows, weight_ref[...], preferred_element_type=F32)
    parts = jnp.concatenate([parts, stats_lanes(total, 0)], axis=1).astype(BF16)
    copy.wait()
    pick = targets(migration_ref).astype(BF16)
    moved = jnp.dot(pick, parts[7 * SLOTS :], preferred_element_type=F32).astype(BF16)
    out_ref[:, :SLOTS] = parts.reshape(8, SLOTS, 512)
    for d in range(8):
        out_ref[d, SLOTS:] = moved


def attention_kernel(
    got_ref, states_ref, retain_ref, listed_ref, out_ref, place_ref, o_ref, migration_ref, sems
):
    (copy,) = fetch([(listed_ref, migration_ref)], sems)
    total = got_ref[0].astype(F32)
    for i in range(1, 8):
        total += got_ref[i].astype(F32)
    squares = total[:, 384:385] + total[:, 385:386]
    scale = lax.rsqrt(squares * (1.0 / D) + EPS)
    q, k, v = (silu(scale * total[:, 128 * i : 128 * i + 128]) for i in range(3))
    rows = SLOTS + MIG
    turned = jnp.concatenate([q, jnp.zeros((128 - rows, 128), F32)], axis=0).T
    for s in range(SLOTS):
        o_ref[s : s + 1, :] = jnp.sum(turned[:, s : s + 1] * states_ref[s], axis=0, keepdims=True)
    copy.wait()
    place_ref[...] = targets(migration_ref).T
    for m in range(MIG):
        s = SLOTS + m
        o_ref[s : s + 1, :] = jnp.sum(
            turned[:, s : s + 1] * states_ref[migration_ref[1, m]], axis=0, keepdims=True
        )
    mixed = retain_ref[:1] * o_ref[...] + jnp.sum(q * k, axis=1, keepdims=True) * v
    heads = mixed * lax.rsqrt(jnp.mean(mixed * mixed, axis=1, keepdims=True) + EPS)
    own, moved = heads[:SLOTS].astype(BF16), heads[SLOTS:]
    row, group = lax.broadcasted_iota(jnp.int32, (MIG, DH), 0), index_of(GRP)
    for m in range(MIG):
        moved = jnp.where((row == m) & (migration_ref[0, m] != group), 0.0, moved)
    moved = moved.astype(BF16)
    for d in range(8):
        out_ref[d, :SLOTS] = own
        out_ref[d, SLOTS:] = moved


def output_kernel(got_ref, weight_ref, place_ref, keep_ref, send_ref):
    first = index_of("c") == 0
    moved = got_ref[0, SLOTS:].astype(F32)
    for i in range(1, 8):
        moved += got_ref[i, SLOTS:].astype(F32)
    place = place_ref[...]
    landed = jnp.dot(place.astype(BF16), moved.astype(BF16), preferred_element_type=F32)
    taken = jnp.sum(place, axis=1, keepdims=True) > 0.0
    last = jnp.where(taken, landed, got_ref[7, :SLOTS].astype(F32)).astype(BF16)
    rows = jnp.concatenate([got_ref[:7, :SLOTS].reshape(7 * SLOTS, DH), last], axis=0)
    part = dot_nt(rows, weight_ref[...])
    low, high = part[:, :HALF], part[:, HALF:]
    keep_ref[...] = jnp.where(first, low, high).reshape(32, 8, HALF)
    send_ref[...] = jnp.where(first, high, low).reshape(32, 8, HALF).astype(BF16)


def resid_kernel(got_ref, tokens_ref, spread_ref):
    total = got_ref[0].astype(F32)
    for i in range(1, 32):
        total += got_ref[i].astype(F32)
    resid = (tokens_ref[...] + total).astype(BF16)
    for i in range(32):
        spread_ref[i] = resid


def gate_kernel(
    own_ref, other_ref, gate_ref, up_ref, router_ref, gain_ref, out_ref, blocks_ref
):
    first = index_of("c") == 0
    own = own_ref[...].astype(F32).reshape(8 * SLOTS, HALF)
    other = other_ref[...].astype(F32).reshape(8 * SLOTS, HALF)
    rows = jnp.concatenate([jnp.where(first, own, other), jnp.where(first, other, own)], axis=1)
    start = lax.broadcasted_iota(jnp.int32, (SLICE, CHUNK), 0) - CHUNK * index_of(("zl", "c"))
    pick = (start == lax.broadcasted_iota(jnp.int32, (SLICE, CHUNK), 1)).astype(F32).astype(BF16)
    blocks = jnp.dot(rows.astype(BF16), pick, preferred_element_type=F32)
    blocks_ref[...] = blocks.astype(BF16).reshape(8, SLOTS, CHUNK)
    rows, total = scaled_rows(rows, gain_ref, index_of(GRP))
    gate = dot_nt(rows, gate_ref[:256])
    up = dot_nt(rows, up_ref[:256])
    at = pl.multiple_of(index_of(GRP) * SLICE, SLICE)
    router = router_ref[:, pl.ds(at, SLICE)]
    rest = jnp.concatenate([gate_ref[256:], up_ref[256:], router, jnp.zeros_like(router)], axis=0)
    tail = dot_nt(rows, rest) + stats_lanes(total, 96)
    out_ref[:, :, :256] = gate.astype(BF16).reshape(8, SLOTS, 256)
    out_ref[:, :, 256:512] = up.astype(BF16).reshape(8, SLOTS, 256)
    out_ref[:, :, 512:640] = tail.astype(BF16).reshape(8, SLOTS, 128)


def hidden_kernel(got_ref, blocks_ref, ids_ref, slot_row_ref, out_ref):
    expert = index_of(EPA) * UNITS // FF
    total = got_ref[0].astype(F32)
    for i in range(1, 8):
        total += got_ref[i].astype(F32)
    tail = total[:, 512:640]
    scale = lax.rsqrt((tail[:, 96:97] + tail[:, 97:98]) * (1.0 / D) + EPS)
    main = silu(scale * total[:, :256]) * (scale * total[:, 256:512])
    rest = silu(scale * tail[:, :32]) * (scale * tail[:, 32:64])
    logits = scale * tail[:, 64:96]
    place = lax.broadcasted_iota(jnp.int32, (SLOTS, SLOTS), 0) == slot_row_ref[...]
    ids = dot_nt(place.astype(F32).astype(BF16), ids_ref[...].astype(F32).astype(BF16))
    ids = (ids + 0.5).astype(jnp.int32)
    at = lax.broadcasted_iota(jnp.int32, (SLOTS, 32), 1)
    lifted = []
    for i in range(2):
        chosen = jnp.sum(jnp.where(at == ids[:, i : i + 1], logits, 0.0), axis=1, keepdims=True)
        lifted.append(1.0 / (1.0 + jnp.exp(-chosen)))
    mine = jnp.where(ids[:, 0:1] == expert, lifted[0], 0.0)
    mine += jnp.where(ids[:, 1:2] == expert, lifted[1], 0.0)
    share = mine / (lifted[0] + lifted[1])
    main, rest = (main * share).astype(BF16), rest * share
    for d in range(8):
        out_ref[d, :, :256] = main
        out_ref[d, :, 256:] = jnp.concatenate([rest, blocks_ref[d].astype(F32)], axis=1).astype(BF16)


def down_kernel(got_ref, down_ref, out_ref, resid_ref):
    part = jnp.dot(
        got_ref[:, :, :UNITS].reshape(8 * SLOTS, UNITS), down_ref[...], preferred_element_type=F32
    )
    resid_ref[...] = got_ref[index_of(("yh", "zh")), :, UNITS:]
    for chunk in range(8):
        rows = part[:, CHUNK * chunk : CHUNK * chunk + CHUNK].reshape(8, SLOTS, CHUNK)
        out_ref[:, chunk % 2, chunk // 2] = packed(rows).astype(BF16)


def pair_kernel(got_ref, out_ref):
    out_ref[...] = (got_ref[:, 0].astype(F32) + got_ref[:, 1].astype(F32)).astype(BF16)


def final_kernel(got_ref, resid_ref, slot_ref, out_ref):
    total = got_ref[0].astype(F32)
    for i in range(1, 32):
        total += got_ref[i].astype(F32)
    out = (resid_ref[...].astype(F32) + unpacked(total)).astype(BF16)
    place = lax.broadcasted_iota(jnp.int32, (SLOTS, SLOTS), 0) == slot_ref[...]
    out_ref[...] = lax.dot_general(
        place.astype(F32).astype(BF16), out, (((0,), (0,)), ((), ())), preferred_element_type=F32
    ).astype(BF16)


def in_hbm(x):
    return pltpu.with_memory_space_constraint(x, pltpu.HBM)


def exchange(x, axes):
    return lax.all_to_all(x, axes, 0, 0)


def shards(
    tokens,
    query_weight,
    key_weight,
    value_weight,
    output_weight,
    gate_weight,
    up_weight,
    down_weight,
    router_weight,
    attn_gain,
    expert_gain,
    decay_rate,
    states,
    expert_ids,
    row_slot,
    migration,
):
    slot_row, migration, expert_ids = row_slot[None, :], migration.T, expert_ids.T
    attn_gain, expert_gain = attn_gain.reshape(48, 128), expert_gain.reshape(48, 128)

    def merge(keep, send):
        return (keep + lax.ppermute(send, "c", CORES).astype(F32)).astype(BF16)

    spread, weight, scale, retain = pl.pallas_call(
        sort_kernel,
        out_shape=(
            pltpu.VMEM((32, *PACK), BF16),
            pltpu.VMEM((SLICE, 3 * DH), BF16),
            pltpu.VMEM((48, 128), F32),
            pltpu.VMEM((8, DH), F32),
        ),
        in_specs=[HBM] * 6 + [VMEM],
        out_specs=(VMEM,) * 4,
        scratch_shapes=[
            pltpu.VMEM((SLOTS, CHUNK), BF16),
            pltpu.VMEM((1, SLOTS), jnp.int32),
            pltpu.SemaphoreType.DMA((6,)),
        ],
        name="sorted_rows",
    )(*map(in_hbm, (tokens, slot_row, query_weight, key_weight, value_weight, attn_gain)), decay_rate[None])
    got = exchange(spread, CHIPS).reshape(8, 1, 4, *PACK)
    got = jnp.broadcast_to(got, (8, 2, 4, *PACK)).reshape(16, 4, *PACK)
    got = exchange(got, GRP + ("c",)).reshape(8, 2, 4, *PACK)
    parts, block = pl.pallas_call(
        qkv_kernel,
        out_shape=(shape((8, SLOTS + MIG, 512), BF16), shape((8, HALF), F32)),
        in_specs=[VMEM, VMEM, VMEM, HBM],
        out_specs=(VMEM, VMEM),
        scratch_shapes=[
            pltpu.VMEM((8 * SLOTS, HALF), F32),
            pltpu.SMEM((3, MIG), jnp.int32),
            pltpu.SemaphoreType.DMA((1,)),
        ],
        compiler_params=pltpu.CompilerParams(vmem_limit_bytes=16 << 20),
        name="qkv_parts",
    )(got, weight, scale, in_hbm(migration))
    parts = exchange(parts, GRP)
    heads, place = pl.pallas_call(
        attention_kernel,
        out_shape=(shape((8, SLOTS + MIG, DH), BF16), shape((SLOTS, MIG), F32)),
        in_specs=[VMEM, VMEM, VMEM, HBM],
        out_specs=(VMEM, VMEM),
        scratch_shapes=[
            pltpu.VMEM((SLOTS + MIG, DH), F32),
            pltpu.SMEM((3, MIG), jnp.int32),
            pltpu.SemaphoreType.DMA((1,)),
        ],
        compiler_params=pltpu.CompilerParams(vmem_limit_bytes=16 << 20),
        name="attention",
    )(parts, states[:, 0], retain, in_hbm(migration))
    heads = exchange(heads, GRP)
    keep, send = call(
        output_kernel,
        (shape((32, 8, HALF), F32), shape((32, 8, HALF), BF16)),
        (heads, output_weight, place),
        "output_parts",
    )
    spread = call(
        resid_kernel,
        shape((32, 8, HALF), BF16),
        (exchange(merge(keep, send), CHIPS), block),
        "resid",
    )
    own = exchange(spread, CHIPS)
    other = lax.ppermute(own, "c", CORES)
    parts, blocks = call(
        gate_kernel,
        (shape((8, SLOTS, 640), BF16), shape((8, SLOTS, CHUNK), BF16)),
        (own, other, gate_weight.T, up_weight.T, router_weight.T, expert_gain),
        "gate_parts",
    )
    parts = exchange(parts, GRP)
    hidden = call(
        hidden_kernel,
        shape((8, SLOTS, UNITS + CHUNK), BF16),
        (parts, blocks, expert_ids, slot_row),
        "hidden",
    )
    hidden = exchange(hidden, GRP)
    parts, resid = call(
        down_kernel,
        (shape((8, 2, 4, *PACK), BF16), shape((SLOTS, CHUNK), BF16)),
        (hidden, down_weight.T),
        "down_parts",
    )
    parts = exchange(parts.reshape(16, 4, *PACK), GRP + ("c",)).reshape(8, 2, 4, *PACK)
    parts = call(pair_kernel, shape((8, 4, *PACK), BF16), (parts,), "pair_sum")
    parts = exchange(parts.reshape(32, *PACK), CHIPS)
    return call(
        final_kernel,
        shape((SLOTS, CHUNK), BF16),
        (parts, resid, slot_row),
        "layer_out",
    )


def solution(mesh):
    fine = jax.sharding.Mesh(
        mesh.devices.reshape(2, 4, 4, 2, 4, 2), ("yl", "x", "yh", "zh", "zl", "c")
    )
    both = P(GRP, EPA)
    placed = (both,) * 8 + (
        P(),
        P(),
        P(),
        P(EPA),
        P(GRP, EPA, None, None),
        P(GRP, None),
        P(GRP),
        P(),
    )
    return jax.shard_map(shards, mesh=fine, in_specs=placed, out_specs=both, check_vma=False)
```

```python
import jax
import jax.numpy as jnp
from jax import lax
from jax.experimental import pallas as pl
from jax.experimental.pallas import tpu as pltpu
from jax.sharding import PartitionSpec as P

BF16, F32 = jnp.bfloat16, jnp.float32
GRP = ("yl", "x")
EPA = ("yh", "zh", "zl", "c")
CHIPS = ("yh", "zh", "zl")
CORES = [(0, 1), (1, 0)]
D, FF, DH = 6144, 9216, 128
EPS = 1e-6
PACK = (24, 128)
CHUNK, HALF, SLICE, SLOTS, MIG, UNITS = 96, 384, 768, 32, 16, 288
VMEM = pl.BlockSpec(memory_space=pltpu.VMEM)
HBM = pl.BlockSpec(memory_space=pltpu.HBM)
SMEM = pl.BlockSpec(memory_space=pltpu.SMEM)


def call(kernel, outs, ins, name, smem=(), limit=16 << 20):
    specs = [SMEM if i in smem else VMEM for i in range(len(ins))]
    return pl.pallas_call(
        kernel,
        out_shape=outs,
        in_specs=specs,
        out_specs=jax.tree.map(lambda _: VMEM, outs),
        compiler_params=pltpu.CompilerParams(vmem_limit_bytes=limit),
        name=name,
    )(*ins)


def index_of(axes):
    return lax.axis_index(axes).astype(jnp.int32)


def shape(dims, dtype):
    return jax.ShapeDtypeStruct(dims, dtype)


def dot_nt(left, right):
    return lax.dot_general(left, right, (((1,), (1,)), ((), ())), preferred_element_type=F32)


def silu(x):
    return x * (1.0 / (1.0 + jnp.exp(-x)))


def packed(rows):
    last = rows[..., 24:, :]
    beside = jnp.concatenate([last[..., 32 * i : 32 * i + 32] for i in range(3)], axis=-2)
    return jnp.concatenate([rows[..., :24, :], beside], axis=-1)


def unpacked(rows):
    beside = rows[..., CHUNK:]
    last = jnp.concatenate([beside[..., 8 * i : 8 * i + 8, :] for i in range(3)], axis=-1)
    return jnp.concatenate([rows[..., :CHUNK], last], axis=-2)


def fetch(pairs, sems):
    copies = [pltpu.make_async_copy(a, b, sems.at[i]) for i, (a, b) in enumerate(pairs)]
    for copy in copies:
        copy.start()
    return copies


def sort_kernel(
    tokens_ref, slot_ref, q_ref, k_ref, v_ref, gain_ref,
    out_ref, weight_ref, scale_ref, held_ref, row_ref, sems,
):
    pairs = [(ref, weight_ref.at[:, pl.ds(128 * i, 128)]) for i, ref in enumerate((q_ref, k_ref, v_ref))]
    tokens, slots, *copies = fetch(
        [(tokens_ref, held_ref), (slot_ref, row_ref), *pairs, (gain_ref, scale_ref)], sems
    )
    tokens.wait()
    slots.wait()
    place = lax.broadcasted_iota(jnp.int32, (SLOTS, SLOTS), 0) == row_ref[...]
    rows = packed(
        jnp.dot(place.astype(F32).astype(BF16), held_ref[...], preferred_element_type=F32)
    ).astype(BF16)
    for i in range(32):
        out_ref[i] = rows
    for copy in copies:
        copy.wait()


def chunk_rows(got_ref):
    return jnp.concatenate(
        [
            unpacked(got_ref[:, core, pair].astype(F32)).reshape(8 * SLOTS, CHUNK)
            for pair in range(4)
            for core in range(2)
        ],
        axis=1,
    )


def scaled_rows(rows, gain_ref, group):
    scaled = [
        (rows[:, 128 * j : 128 * j + 128] * gain_ref[pl.ds(6 * group + j, 1), :]).astype(BF16)
        for j in range(6)
    ]
    return jnp.concatenate(scaled, axis=1), jnp.sum(rows * rows, axis=1, keepdims=True)


def stats_lanes(total, lane):
    high = total.astype(BF16).astype(F32)
    at = lax.broadcasted_iota(jnp.int32, (total.shape[0], 128), 1)
    return jnp.where(at == lane, high, jnp.where(at == lane + 1, total - high, 0.0))


def targets(migration_ref):
    row = lax.broadcasted_iota(jnp.int32, (MIG, SLOTS), 0)
    slot = lax.broadcasted_iota(jnp.int32, (MIG, SLOTS), 1)
    found = jnp.zeros((MIG, SLOTS), F32)
    for m in range(MIG):
        found = jnp.where((row == m) & (slot == migration_ref[2, m]), 1.0, found)
    return found


def qkv_kernel(
    got_ref, weight_ref, scale_ref, listed_ref, decay_ref, out_ref, tokens_ref, retain_ref, half_ref, migration_ref, sems
):
    (copy,) = fetch([(listed_ref, migration_ref)], sems)
    first = index_of("c") == 0
    rows = chunk_rows(got_ref)
    half_ref[...] = jnp.where(first, rows[:, :HALF], rows[:, HALF:])
    tokens_ref[...] = half_ref[pl.ds(pl.multiple_of(8 * index_of(CHIPS), 8), 8), :]
    rows, total = scaled_rows(rows, scale_ref, index_of(GRP))
    retain_ref[...] = jnp.broadcast_to(jnp.exp(-decay_ref[...]), retain_ref.shape)
    parts = jnp.dot(rows, weight_ref[...], preferred_element_type=F32)
    parts = jnp.concatenate([parts, stats_lanes(total, 0)], axis=1).astype(BF16)
    copy.wait()
    pick = targets(migration_ref).astype(BF16)
    moved = jnp.dot(pick, parts[7 * SLOTS :], preferred_element_type=F32).astype(BF16)
    out_ref[:, :SLOTS] = parts.reshape(8, SLOTS, 512)
    for d in range(8):
        out_ref[d, SLOTS:] = moved


def attention_kernel(
    got_ref, states_ref, retain_ref, listed_ref, out_ref, place_ref, o_ref, migration_ref, sems
):
    (copy,) = fetch([(listed_ref, migration_ref)], sems)
    total = got_ref[0].astype(F32)
    for i in range(1, 8):
        total += got_ref[i].astype(F32)
    squares = total[:, 384:385] + total[:, 385:386]
    scale = lax.rsqrt(squares * (1.0 / D) + EPS)
    q, k, v = (silu(scale * total[:, 128 * i : 128 * i + 128]) for i in range(3))
    rows = SLOTS + MIG
    turned = jnp.concatenate([q, jnp.zeros((128 - rows, 128), F32)], axis=0).T
    for s in range(SLOTS):
        o_ref[s : s + 1, :] = jnp.sum(turned[:, s : s + 1] * states_ref[s], axis=0, keepdims=True)
    copy.wait()
    place_ref[...] = targets(migration_ref).T
    for m in range(MIG):
        s = SLOTS + m
        o_ref[s : s + 1, :] = jnp.sum(
            turned[:, s : s + 1] * states_ref[migration_ref[1, m]], axis=0, keepdims=True
        )
    mixed = retain_ref[:1] * o_ref[...] + jnp.sum(q * k, axis=1, keepdims=True) * v
    heads = mixed * lax.rsqrt(jnp.mean(mixed * mixed, axis=1, keepdims=True) + EPS)
    own, moved = heads[:SLOTS].astype(BF16), heads[SLOTS:]
    row, group = lax.broadcasted_iota(jnp.int32, (MIG, DH), 0), index_of(GRP)
    for m in range(MIG):
        moved = jnp.where((row == m) & (migration_ref[0, m] != group), 0.0, moved)
    moved = moved.astype(BF16)
    for d in range(8):
        out_ref[d, :SLOTS] = own
        out_ref[d, SLOTS:] = moved


def output_kernel(got_ref, weight_ref, place_ref, keep_ref, send_ref):
    first = index_of("c") == 0
    moved = got_ref[0, SLOTS:].astype(F32)
    for i in range(1, 8):
        moved += got_ref[i, SLOTS:].astype(F32)
    place = place_ref[...]
    landed = jnp.dot(place.astype(BF16), moved.astype(BF16), preferred_element_type=F32)
    taken = jnp.sum(place, axis=1, keepdims=True) > 0.0
    last = jnp.where(taken, landed, got_ref[7, :SLOTS].astype(F32)).astype(BF16)
    rows = jnp.concatenate([got_ref[:7, :SLOTS].reshape(7 * SLOTS, DH), last], axis=0)
    part = dot_nt(rows, weight_ref[...])
    low, high = part[:, :HALF], part[:, HALF:]
    keep_ref[...] = jnp.where(first, low, high).reshape(32, 8, HALF)
    send_ref[...] = jnp.where(first, high, low).reshape(32, 8, HALF).astype(BF16)


def resid_kernel(got_ref, tokens_ref, spread_ref):
    total = got_ref[0].astype(F32)
    for i in range(1, 32):
        total += got_ref[i].astype(F32)
    resid = (tokens_ref[...] + total).astype(BF16)
    for i in range(32):
        spread_ref[i] = resid


def gate_kernel(
    own_ref, other_ref, gate_ref, up_ref, router_ref, gain_ref, out_ref, blocks_ref
):
    first = index_of("c") == 0
    own = own_ref[...].astype(F32).reshape(8 * SLOTS, HALF)
    other = other_ref[...].astype(F32).reshape(8 * SLOTS, HALF)
    rows = jnp.concatenate([jnp.where(first, own, other), jnp.where(first, other, own)], axis=1)
    start = lax.broadcasted_iota(jnp.int32, (SLICE, CHUNK), 0) - CHUNK * index_of(("zl", "c"))
    pick = (start == lax.broadcasted_iota(jnp.int32, (SLICE, CHUNK), 1)).astype(F32).astype(BF16)
    blocks = jnp.dot(rows.astype(BF16), pick, preferred_element_type=F32)
    blocks_ref[...] = blocks.astype(BF16).reshape(8, SLOTS, CHUNK)
    rows, total = scaled_rows(rows, gain_ref, index_of(GRP))
    gate = dot_nt(rows, gate_ref[:256])
    up = dot_nt(rows, up_ref[:256])
    at = pl.multiple_of(index_of(GRP) * SLICE, SLICE)
    router = router_ref[:, pl.ds(at, SLICE)]
    rest = jnp.concatenate([gate_ref[256:], up_ref[256:], router, jnp.zeros_like(router)], axis=0)
    tail = dot_nt(rows, rest) + stats_lanes(total, 96)
    out_ref[:, :, :256] = gate.astype(BF16).reshape(8, SLOTS, 256)
    out_ref[:, :, 256:512] = up.astype(BF16).reshape(8, SLOTS, 256)
    out_ref[:, :, 512:640] = tail.astype(BF16).reshape(8, SLOTS, 128)


def hidden_kernel(got_ref, blocks_ref, ids_ref, slot_row_ref, out_ref):
    expert = index_of(EPA) * UNITS // FF
    total = got_ref[0].astype(F32)
    for i in range(1, 8):
        total += got_ref[i].astype(F32)
    tail = total[:, 512:640]
    scale = lax.rsqrt((tail[:, 96:97] + tail[:, 97:98]) * (1.0 / D) + EPS)
    main = silu(scale * total[:, :256]) * (scale * total[:, 256:512])
    rest = silu(scale * tail[:, :32]) * (scale * tail[:, 32:64])
    logits = scale * tail[:, 64:96]
    place = lax.broadcasted_iota(jnp.int32, (SLOTS, SLOTS), 0) == slot_row_ref[...]
    ids = dot_nt(place.astype(F32).astype(BF16), ids_ref[...].astype(F32).astype(BF16))
    ids = (ids + 0.5).astype(jnp.int32)
    at = lax.broadcasted_iota(jnp.int32, (SLOTS, 32), 1)
    lifted = []
    for i in range(2):
        chosen = jnp.sum(jnp.where(at == ids[:, i : i + 1], logits, 0.0), axis=1, keepdims=True)
        lifted.append(1.0 / (1.0 + jnp.exp(-chosen)))
    mine = jnp.where(ids[:, 0:1] == expert, lifted[0], 0.0)
    mine += jnp.where(ids[:, 1:2] == expert, lifted[1], 0.0)
    share = mine / (lifted[0] + lifted[1])
    main, rest = (main * share).astype(BF16), rest * share
    for d in range(8):
        out_ref[d, :, :256] = main
        out_ref[d, :, 256:] = jnp.concatenate([rest, blocks_ref[d].astype(F32)], axis=1).astype(BF16)


def down_kernel(got_ref, down_ref, out_ref, resid_ref):
    part = jnp.dot(
        got_ref[:, :, :UNITS].reshape(8 * SLOTS, UNITS), down_ref[...], preferred_element_type=F32
    )
    resid_ref[...] = got_ref[index_of(("yh", "zh")), :, UNITS:]
    for chunk in range(8):
        rows = part[:, CHUNK * chunk : CHUNK * chunk + CHUNK].reshape(8, SLOTS, CHUNK)
        out_ref[:, chunk % 2, chunk // 2] = packed(rows).astype(BF16)


def pair_kernel(got_ref, out_ref):
    out_ref[...] = (got_ref[:, 0].astype(F32) + got_ref[:, 1].astype(F32)).astype(BF16)


def final_kernel(got_ref, resid_ref, slot_ref, out_ref):
    total = got_ref[0].astype(F32)
    for i in range(1, 32):
        total += got_ref[i].astype(F32)
    out = (resid_ref[...].astype(F32) + unpacked(total)).astype(BF16)
    place = lax.broadcasted_iota(jnp.int32, (SLOTS, SLOTS), 0) == slot_ref[...]
    out_ref[...] = lax.dot_general(
        place.astype(F32).astype(BF16), out, (((0,), (0,)), ((), ())), preferred_element_type=F32
    ).astype(BF16)


def in_hbm(x):
    return pltpu.with_memory_space_constraint(x, pltpu.HBM)


def exchange(x, axes):
    return lax.all_to_all(x, axes, 0, 0)


def shards(
    tokens,
    query_weight,
    key_weight,
    value_weight,
    output_weight,
    gate_weight,
    up_weight,
    down_weight,
    router_weight,
    attn_gain,
    expert_gain,
    decay_rate,
    states,
    expert_ids,
    row_slot,
    migration,
):
    slot_row, migration, expert_ids = row_slot[None, :], migration.T, expert_ids.T
    attn_gain, expert_gain = attn_gain.reshape(48, 128), expert_gain.reshape(48, 128)

    def merge(keep, send):
        return (keep + lax.ppermute(send, "c", CORES).astype(F32)).astype(BF16)

    spread, weight, scale = pl.pallas_call(
        sort_kernel,
        out_shape=(
            pltpu.VMEM((32, *PACK), BF16),
            pltpu.VMEM((SLICE, 3 * DH), BF16),
            pltpu.VMEM((48, 128), F32),
        ),
        in_specs=[HBM] * 6,
        out_specs=(VMEM,) * 3,
        scratch_shapes=[
            pltpu.VMEM((SLOTS, CHUNK), BF16),
            pltpu.VMEM((1, SLOTS), jnp.int32),
            pltpu.SemaphoreType.DMA((6,)),
        ],
        name="sorted_rows",
    )(*map(in_hbm, (tokens, slot_row, query_weight, key_weight, value_weight, attn_gain)))
    got = exchange(spread, CHIPS).reshape(8, 1, 4, *PACK)
    got = jnp.broadcast_to(got, (8, 2, 4, *PACK)).reshape(16, 4, *PACK)
    got = exchange(got, GRP + ("c",)).reshape(8, 2, 4, *PACK)
    parts, block, retain = pl.pallas_call(
        qkv_kernel,
        out_shape=(shape((8, SLOTS + MIG, 512), BF16), shape((8, HALF), F32), shape((8, DH), F32)),
        in_specs=[VMEM, VMEM, VMEM, HBM, VMEM],
        out_specs=(VMEM,) * 3,
        scratch_shapes=[
            pltpu.VMEM((8 * SLOTS, HALF), F32),
            pltpu.SMEM((3, MIG), jnp.int32),
            pltpu.SemaphoreType.DMA((1,)),
        ],
        compiler_params=pltpu.CompilerParams(vmem_limit_bytes=16 << 20),
        name="qkv_parts",
    )(got, weight, scale, in_hbm(migration), decay_rate[None])
    parts = exchange(parts, GRP)
    heads, place = pl.pallas_call(
        attention_kernel,
        out_shape=(shape((8, SLOTS + MIG, DH), BF16), shape((SLOTS, MIG), F32)),
        in_specs=[VMEM, VMEM, VMEM, HBM],
        out_specs=(VMEM, VMEM),
        scratch_shapes=[
            pltpu.VMEM((SLOTS + MIG, DH), F32),
            pltpu.SMEM((3, MIG), jnp.int32),
            pltpu.SemaphoreType.DMA((1,)),
        ],
        compiler_params=pltpu.CompilerParams(vmem_limit_bytes=16 << 20),
        name="attention",
    )(parts, states[:, 0], retain, in_hbm(migration))
    heads = exchange(heads, GRP)
    keep, send = call(
        output_kernel,
        (shape((32, 8, HALF), F32), shape((32, 8, HALF), BF16)),
        (heads, output_weight, place),
        "output_parts",
    )
    spread = call(
        resid_kernel,
        shape((32, 8, HALF), BF16),
        (exchange(merge(keep, send), CHIPS), block),
        "resid",
    )
    own = exchange(spread, CHIPS)
    other = lax.ppermute(own, "c", CORES)
    parts, blocks = call(
        gate_kernel,
        (shape((8, SLOTS, 640), BF16), shape((8, SLOTS, CHUNK), BF16)),
        (own, other, gate_weight.T, up_weight.T, router_weight.T, expert_gain),
        "gate_parts",
    )
    parts = exchange(parts, GRP)
    hidden = call(
        hidden_kernel,
        shape((8, SLOTS, UNITS + CHUNK), BF16),
        (parts, blocks, expert_ids, slot_row),
        "hidden",
    )
    hidden = exchange(hidden, GRP)
    parts, resid = call(
        down_kernel,
        (shape((8, 2, 4, *PACK), BF16), shape((SLOTS, CHUNK), BF16)),
        (hidden, down_weight.T),
        "down_parts",
    )
    parts = exchange(parts.reshape(16, 4, *PACK), GRP + ("c",)).reshape(8, 2, 4, *PACK)
    parts = call(pair_kernel, shape((8, 4, *PACK), BF16), (parts,), "pair_sum")
    parts = exchange(parts.reshape(32, *PACK), CHIPS)
    return call(
        final_kernel,
        shape((SLOTS, CHUNK), BF16),
        (parts, resid, slot_row),
        "layer_out",
    )


def solution(mesh):
    fine = jax.sharding.Mesh(
        mesh.devices.reshape(2, 4, 4, 2, 4, 2), ("yl", "x", "yh", "zh", "zl", "c")
    )
    both = P(GRP, EPA)
    placed = (both,) * 8 + (
        P(),
        P(),
        P(),
        P(EPA),
        P(GRP, EPA, None, None),
        P(GRP, None),
        P(GRP),
        P(),
    )
    return jax.shard_map(shards, mesh=fine, in_specs=placed, out_specs=both, check_vma=False)
```
